32 devices in a mesh: grid: 8 (over z, y), tm: 2 (over core), pw: 2 (over x).
Axes of the slice: x: 2, y: 2, z: 4, core: 2. Of those that a mesh axis runs over, the one named last changes fastest.
Arguments:
- slab_orbitals: bfloat16 [8, 896, 512], P('grid'), may hold values from -6 to 6
- orbital_block: int32 [8], replicated, may hold values from 0 to 7, each once
- occupied_columns: bfloat16 [1024, 16, 4096], P(None, 'pw', 'grid'), may hold values from -0.1875 to 0.1875
- unoccupied_columns: bfloat16 [6144, 16, 4096], P(None, 'pw', 'grid'), may hold values from -0.078125 to 0.078125
- occupied_gap: float32 [1024], replicated, may hold values from 0.02 to 1
- unoccupied_gap: float32 [6144], replicated, may hold values from 0.02 to 2
- time_table: float32 [16], replicated, may hold values from 0.05 to 2
- frequency_table: float32 [16], replicated, may hold values from 0.1 to 4
- time_weight: float32 [16], replicated, may hold values from 1 to 4
- time_index: int32 [2], replicated, may hold values from 0 to 15
- frequency_index: int32 [2], replicated, may hold values from 0 to 15
Outputs:
- polarizability: float32 [2, 512, 16, 64, 128], P('tm', ('grid', 'pw'))
The draws below stay inside these ranges and needn't reach their ends.
Inputs may be any that keep to these rules, and one draw needn't show every extreme that they name: orbital_block names each block 0 to 7 exactly once.
All inputs are finite; a program needn't handle non-finite values.
Results may differ from the reference program's by a relative error of at most 0.0051.
Values may be sent and summed in bfloat16 or wider, within the bound.
No kernel may reach another device: no remote copies, remote signals or barrier semaphores. Data moves between devices by JAX's collectives and lax.ppermute only.
A program may use at most 256 MiB of HBM per device.

```python
import math
import jax
import jax.numpy as jnp
from jax import lax

NOCC = 1024
NVIR = 6144
NX = 64
NY = 64
NTAU = 16
SLAB = 512
NBLK = 8
NPAIR = 2
NZW = 16
BLOCK_ROWS = 896


def block_scale(rng, dims, cuts, least, high):
    level = 1.0
    for position, shards_of in cuts:
        heights = jax.random.uniform(jax.random.fold_in(jax.random.fold_in(rng, 6), position), (shards_of,), jnp.float32, least / len(cuts), high / len(cuts))
        level = level * jnp.repeat(jnp.exp(heights), dims[position] // shards_of).reshape((-1,) + (1,) * (len(dims) - 1 - position))
    return level


def bell_draw(rng, extent, scale, limit, cuts=(), kind=jnp.bfloat16):
    loudness = block_scale(rng, extent, cuts, -0.22, 0.18) if cuts else 1.0
    array = jax.random.normal(rng, extent, jnp.float32) * scale * loudness
    return jnp.minimum(jnp.maximum(array, -limit), limit).astype(kind)


def setup_inputs(seed: int = 0) -> dict:
    seeds = jax.random.split(jax.random.key(seed), 12)
    slab_orbitals = bell_draw(seeds[0], (NBLK, BLOCK_ROWS, SLAB), 1.0, 6.0, ((0, 8),))
    orbital_block = jax.random.permutation(seeds[1], NBLK).astype(jnp.int32)
    occupied_columns = bell_draw(seeds[2], (NOCC, NZW, NY * NX), NOCC ** -0.5, 0.1875, ((1, 2), (2, 8)))
    unoccupied_columns = bell_draw(seeds[3], (NVIR, NZW, NY * NX), NVIR ** -0.5, 0.078125, ((1, 2), (2, 8)))
    occupied_gap = jnp.clip(jnp.exp(jax.random.uniform(seeds[4], (NOCC,), jnp.float32, math.log(0.02), math.log(1.0))), 0.02, 1.0)
    unoccupied_gap = jnp.clip(jnp.exp(jax.random.uniform(seeds[5], (NVIR,), jnp.float32, math.log(0.02), math.log(2.0))), 0.02, 2.0)
    time_table = jnp.clip(jnp.exp(jax.random.uniform(seeds[6], (NTAU,), jnp.float32, math.log(0.05), math.log(2.0))), 0.05, 2.0)
    frequency_table = jnp.clip(jnp.exp(jax.random.uniform(seeds[7], (NTAU,), jnp.float32, math.log(0.1), math.log(4.0))), 0.1, 4.0)
    time_weight = jnp.clip(jnp.exp(jax.random.uniform(seeds[8], (NTAU,), jnp.float32, math.log(1.0), math.log(4.0))), 1.0, 4.0)
    time_index = jax.random.randint(seeds[9], (NPAIR,), 0, NTAU).astype(jnp.int32)
    frequency_index = jax.random.randint(seeds[10], (NPAIR,), 0, NTAU).astype(jnp.int32)
    return dict(slab_orbitals=slab_orbitals, orbital_block=orbital_block, occupied_columns=occupied_columns, unoccupied_columns=unoccupied_columns, occupied_gap=occupied_gap, unoccupied_gap=unoccupied_gap, time_table=time_table, frequency_table=frequency_table, time_weight=time_weight, time_index=time_index, frequency_index=frequency_index)


def dft_angles(number):
    indices = jnp.arange(number, dtype=jnp.int32)
    product = indices[:, None] * indices[None, :] % number
    return product.astype(jnp.float32) * (2.0 * math.pi / number)

def row_table(number):
    angles = dft_angles(number)
    factor = 1.0 / math.sqrt(number)
    return jnp.concatenate([jnp.cos(angles), -jnp.sin(angles)], axis=1) * factor

def column_table(number):
    angles = dft_angles(number)
    factor = 1.0 / math.sqrt(number)
    return (jnp.concatenate([jnp.cos(angles), jnp.sin(angles)], axis=0) * factor).astype(jnp.bfloat16)

def combine_parts(y_parts, width_y, width_x):
    cosine = y_parts[..., :width_y, :]
    sine = y_parts[..., width_y:, :]
    real_part = cosine[..., :width_x] + sine[..., width_x:]
    imag_part = cosine[..., width_x:] - sine[..., :width_x]
    return jnp.concatenate([real_part, imag_part], axis=-1)

def reference(slab_orbitals, orbital_block, occupied_columns, unoccupied_columns, occupied_gap, unoccupied_gap, time_table, frequency_table, time_weight, time_index, frequency_index):
    block_count = slab_orbitals.shape[0]
    occupied_count = occupied_columns.shape[0]
    unoccupied_count = unoccupied_columns.shape[0]
    occupied_block = occupied_count // block_count
    canonical = jnp.zeros_like(slab_orbitals).at[orbital_block].set(slab_orbitals)
    occupied_rows = canonical[:, :occupied_block, :].reshape(occupied_count, SLAB)
    unoccupied_rows = canonical[:, occupied_block:, :].reshape(unoccupied_count, SLAB)
    time_points = time_table[time_index]
    occupied_weighted = (occupied_rows[None, :, :] * jnp.exp(-occupied_gap[None, :] * time_points[:, None])[:, :, None]).astype(jnp.bfloat16)
    unoccupied_weighted = (unoccupied_rows[None, :, :] * jnp.exp(-unoccupied_gap[None, :] * time_points[:, None])[:, :, None]).astype(jnp.bfloat16)
    frequency_weights = time_weight[time_index][None, :] * jnp.cos(frequency_table[frequency_index][:, None] * time_points[None, :])
    x_table = row_table(NX)
    y_table = column_table(NY).astype(jnp.float32)

    def one_plane(plane_index):
        occupied_plane = lax.dynamic_index_in_dim(occupied_columns, plane_index, 1, keepdims=False)
        unoccupied_plane = lax.dynamic_index_in_dim(unoccupied_columns, plane_index, 1, keepdims=False)
        summed = jnp.zeros((NPAIR, SLAB, NY, 2 * NX), jnp.float32)
        for moment in range(NPAIR):
            green_occupied = jnp.dot(occupied_weighted[moment].T, occupied_plane, preferred_element_type=jnp.float32)
            green_unoccupied = jnp.dot(unoccupied_weighted[moment].T, unoccupied_plane, preferred_element_type=jnp.float32)
            response = (-green_occupied * green_unoccupied).reshape(SLAB, NY, NX)
            x_transform = jnp.dot(response, x_table, precision=lax.Precision.HIGHEST).astype(jnp.bfloat16)
            y_parts = jnp.einsum('ky,ryc->rkc', y_table, x_transform.astype(jnp.float32), precision=lax.Precision.HIGHEST)
            plane_waves = combine_parts(y_parts, NY, NX)
            summed = summed + frequency_weights[:, moment][:, None, None, None] * plane_waves[None]
        return summed
    planes = lax.map(one_plane, jnp.arange(NZW, dtype=jnp.int32))
    return jnp.transpose(planes, (1, 2, 0, 3, 4))
```

```python
import math

import jax
import jax.numpy as jnp
import ml_dtypes
import numpy as np
from jax import lax
from jax.experimental import pallas as pl
from jax.experimental.pallas import tpu as pltpu
from jax.sharding import PartitionSpec as P

NX = 64
NY = 64
SLAB = 512


def dft_angles(number):
    indices = jnp.arange(number, dtype=jnp.int32)
    product = indices[:, None] * indices[None, :] % number
    return product.astype(jnp.float32) * (2.0 * math.pi / number)


def row_table(number):
    angles = dft_angles(number)
    factor = 1.0 / math.sqrt(number)
    return jnp.concatenate([jnp.cos(angles), -jnp.sin(angles)], axis=1) * factor


def column_table(number):
    angles = dft_angles(number)
    factor = 1.0 / math.sqrt(number)
    return (jnp.concatenate([jnp.cos(angles), jnp.sin(angles)], axis=0) * factor).astype(
        jnp.bfloat16
    )


def combine_parts(y_parts, width_y, width_x):
    cosine = y_parts[..., :width_y, :]
    sine = y_parts[..., width_y:, :]
    real_part = cosine[..., :width_x] + sine[..., width_x:]
    imag_part = cosine[..., width_x:] - sine[..., :width_x]
    return jnp.concatenate([real_part, imag_part], axis=-1)


def weigh_rows(values, rates, time_point):
    return (values * jnp.exp(-rates * time_point)[:, :, None]).astype(jnp.bfloat16)


def general_shards(
    slab_orbitals,
    orbital_block,
    occupied_columns,
    unoccupied_columns,
    occupied_gap,
    unoccupied_gap,
    time_table,
    frequency_table,
    time_weight,
    time_index,
    frequency_index,
):
    block_count = lax.axis_size("grid")
    occupied_block = occupied_columns.shape[0] // block_count
    unoccupied_block = unoccupied_columns.shape[0] // block_count
    planes_local = occupied_columns.shape[1]
    lines_local = occupied_columns.shape[2] // NX
    width = planes_local * occupied_columns.shape[2]
    occupied_blocks = occupied_columns.reshape(block_count, occupied_block, width)
    unoccupied_blocks = unoccupied_columns.reshape(block_count, unoccupied_block, width)
    occupied_rates = occupied_gap.reshape(block_count, occupied_block)
    unoccupied_rates = unoccupied_gap.reshape(block_count, unoccupied_block)
    moment = lax.axis_index("tm")
    time_slot = time_index[moment]
    time_point = time_table[time_slot]
    frequency_weights = time_weight[time_slot] * jnp.cos(
        frequency_table[frequency_index] * time_point
    )
    pieces = lax.all_gather(slab_orbitals, "grid", axis=0, tiled=True)
    occupied_part = weigh_rows(
        pieces[:, :occupied_block, :], jnp.take(occupied_rates, orbital_block, axis=0), time_point
    )
    unoccupied_part = weigh_rows(
        pieces[:, occupied_block:, :], jnp.take(unoccupied_rates, orbital_block, axis=0), time_point
    )
    green_occupied = jnp.einsum(
        "jis,jic->sc",
        occupied_part,
        jnp.take(occupied_blocks, orbital_block, axis=0),
        preferred_element_type=jnp.float32,
    )
    green_unoccupied = jnp.einsum(
        "jis,jic->sc",
        unoccupied_part,
        jnp.take(unoccupied_blocks, orbital_block, axis=0),
        preferred_element_type=jnp.float32,
    )
    green_occupied, green_unoccupied = (green_occupied, green_unoccupied)
    response = -green_occupied * green_unoccupied
    response = response.reshape(SLAB, planes_local, lines_local, NX)
    tiles = jnp.dot(response, row_table(NX), precision=lax.Precision.HIGHEST).astype(jnp.bfloat16)
    y_table = column_table(NY)
    received = lax.all_to_all(
        tiles[:, None], ("grid", "pw"), split_axis=0, concat_axis=1, tiled=True
    )
    stacked = received[None]
    sources = stacked.reshape(
        stacked.shape[0],
        stacked.shape[1],
        block_count,
        lax.axis_size("pw"),
        planes_local,
        lines_local,
        2 * NX,
    )
    y_parts = jnp.einsum(
        "kgy,trgpzyc->trpzkc",
        y_table.reshape(2 * NY, block_count, lines_local),
        sources,
        preferred_element_type=jnp.float32,
    )
    y_parts = y_parts.reshape(
        y_parts.shape[0], y_parts.shape[1], lax.axis_size("pw") * planes_local, 2 * NY, 2 * NX
    )
    plane_waves = combine_parts(y_parts, NY, NX)
    summed = lax.psum(frequency_weights[:, None, None, None, None] * plane_waves[0][None], "tm")
    return lax.dynamic_slice_in_dim(summed, moment, 1, 0)


PAIR_CHUNKS = (1, 2, 1)
DEPTH = 1024
SPLIT_CALLS = 3
GROUP = 16
VMEM_LIMIT = 56 * 2**20
AXES = ("grid", "tm", "pw")
SWAP = [(0, 1), (1, 0)]


def host_angles(number):
    indices = np.arange(number)
    return (indices[:, None] * indices[None, :] % number) * (2.0 * math.pi / number)


def line_operator(lines):
    angles = host_angles(lines)
    table = np.concatenate([np.cos(angles), np.sin(angles)]) / math.sqrt(lines)
    return table.astype(np.float32).astype(ml_dtypes.bfloat16)


def row_operator(number):
    angles = host_angles(number)
    cosine, sine = np.cos(angles) / math.sqrt(number), np.sin(angles) / math.sqrt(number)
    one = np.stack([np.concatenate([cosine, -sine], 1), np.concatenate([-sine, -cosine], 1)])
    both = np.einsum("sxc,pq->spxqc", one, np.eye(2)).reshape(4 * number, 4 * number)
    high = both.astype(np.float32).astype(ml_dtypes.bfloat16)
    low = (both - high.astype(np.float64)).astype(np.float32).astype(ml_dtypes.bfloat16)
    return high, low


def expected(flops, read_and_written):
    return pl.CostEstimate(flops=flops, bytes_accessed=read_and_written, transcendentals=0)


def split_planes(columns, core, first, steps, previous):
    count, planes, width = columns.shape
    half = width // 2
    pieces = [2 * pairs for pairs in PAIR_CHUNKS]
    group = 256 // planes

    def kernel(core_ref, in_ref, *rest):
        out_refs = rest[-len(pieces) :]
        rows = lax.broadcasted_iota(jnp.int32, (256, 256), 0)
        cols = lax.broadcasted_iota(jnp.int32, (256, 256), 1)
        order = jnp.where((rows % group) * planes + rows // group == cols, 1.0, 0.0)
        order = order.astype(jnp.bfloat16)
        for b in range(DEPTH // group):
            part = in_ref[b * group : (b + 1) * group].reshape(256, half)
            moved = jnp.dot(order, part, preferred_element_type=jnp.float32)
            moved = moved.astype(jnp.bfloat16).reshape(planes, group, half)
            start = 0
            for out_ref, size in zip(out_refs, pieces):
                out_ref[:, b * group : (b + 1) * group, :] = moved[start : start + size]
                start += size

    operands, extra, aliases = [core, columns], [], {}
    if previous is not None:
        operands += previous
        extra = [pl.BlockSpec(memory_space=pl.ANY)] * len(pieces)
        aliases = {2 + n: n for n in range(len(pieces))}
    return pl.pallas_call(
        kernel,
        grid_spec=pltpu.PrefetchScalarGridSpec(
            num_scalar_prefetch=1,
            grid=(steps,),
            in_specs=[pl.BlockSpec((DEPTH, planes, half), lambda i, core: (first + i, 0, core[0]))] + extra,
            out_specs=[pl.BlockSpec((size, DEPTH, half), lambda i, core: (0, first + i, 0)) for size in pieces],
        ),
        out_shape=[jax.ShapeDtypeStruct((size, count, half), jnp.bfloat16) for size in pieces],
        input_output_aliases=aliases,
        compiler_params=pltpu.CompilerParams(vmem_limit_bytes=VMEM_LIMIT),
        cost_estimate=expected(steps * DEPTH * planes * half * 512, steps * DEPTH * planes * half * 4),
        name="split_planes",
    )(*operands)


def weigh(pieces, places, core, decays, previous):
    occupied_decay, unoccupied_decay = decays
    times, occupied_count = occupied_decay.shape
    unoccupied_count = unoccupied_decay.shape[1]
    flat = [entry for block in pieces for entry in block]
    half = SLAB // 2
    width = flat[0][0].shape[1]
    occupied_block = occupied_count * width // (occupied_count + unoccupied_count)
    unoccupied_block = width - occupied_block

    def kernel(place_ref, core_ref, occ_ref, unocc_ref, *rest):
        refs, (occ_out, unocc_out) = list(rest[: len(flat)]), rest[-2:]
        for n, block in enumerate(pieces):
            mine, refs = refs[: len(block)], refs[len(block) :]

            @pl.when(pl.program_id(0) == n)
            def _():
                for ref, (array, other, start) in zip(mine, block):
                    side = 1 - core_ref[0] if other else core_ref[0]
                    at = pl.ds(pl.multiple_of(side * half + start, GROUP), array.shape[0])
                    values = ref[...].astype(jnp.float32)
                    for t in range(times):
                        occ_out[t, at, :] = (values[:, :occupied_block] * occ_ref[t : t + 1, :]).astype(jnp.bfloat16)
                        unocc_out[t, at, :] = (values[:, occupied_block:] * unocc_ref[t : t + 1, :]).astype(jnp.bfloat16)

    operands = [places, core, occupied_decay, unoccupied_decay] + [entry[0] for entry in flat]
    extra, aliases = [], {}
    if previous is not None:
        aliases = {len(operands): 0, len(operands) + 1: 1}
        operands += previous
        extra = [pl.BlockSpec(memory_space=pl.ANY)] * 2
    elements = sum(entry[0].size for entry in flat)
    return pl.pallas_call(
        kernel,
        grid_spec=pltpu.PrefetchScalarGridSpec(
            num_scalar_prefetch=2,
            grid=(len(pieces),),
            in_specs=[
                pl.BlockSpec((times, occupied_block), lambda n, place, core: (0, place[n])),
                pl.BlockSpec((times, unoccupied_block), lambda n, place, core: (0, place[n])),
            ]
            + [pl.BlockSpec(entry[0].shape, lambda n, place, core: (0, 0)) for entry in flat]
            + extra,
            out_specs=[
                pl.BlockSpec((times, 2 * half, occupied_block), lambda n, place, core: (0, 0, place[n])),
                pl.BlockSpec((times, 2 * half, unoccupied_block), lambda n, place, core: (0, 0, place[n])),
            ],
        ),
        out_shape=[
            jax.ShapeDtypeStruct((times, 2 * half, occupied_count), jnp.bfloat16),
            jax.ShapeDtypeStruct((times, 2 * half, unoccupied_count), jnp.bfloat16),
        ],
        input_output_aliases=aliases,
        compiler_params=pltpu.CompilerParams(vmem_limit_bytes=VMEM_LIMIT),
        cost_estimate=expected(elements * 2, elements * 6),
        name="weigh",
    )(*operands)


def respond(weights, occupied, unoccupied, occupied_planes, unoccupied_planes, owners):
    times, slab, occupied_count = occupied.shape
    planes, unoccupied_count, width = unoccupied_planes.shape
    lines = width // NX
    grid_size, pw_size = owners
    rows = slab // (grid_size * pw_size)
    steps = unoccupied_count // DEPTH

    def kernel(weight_ref, occ_ref, unocc_ref, occ_col_ref, unocc_col_ref, out_ref, occ_acc, unocc_acc):
        step = pl.program_id(0)

        @pl.when(step == 0)
        def _():
            unocc_acc[...] = jnp.zeros_like(unocc_acc)
            left = occ_ref[...].reshape(times * slab, occupied_count)
            for z in range(planes):
                occ_acc[z] = jnp.dot(left, occ_col_ref[z], preferred_element_type=jnp.float32)

        left = unocc_ref[...].reshape(times * slab, DEPTH)
        for z in range(planes):
            unocc_acc[z] += jnp.dot(left, unocc_col_ref[z], preferred_element_type=jnp.float32)

        @pl.when(step == steps - 1)
        def _():
            for pair in range(planes // 2):
                mixed = []
                for z in (2 * pair, 2 * pair + 1):
                    product = occ_acc[z] * unocc_acc[z]
                    first, second = product[:slab], product[slab:]
                    mixed.append([
                        (weight_ref[f, 0] * first + weight_ref[f, 1] * second).astype(jnp.bfloat16)
                        for f in range(times)
                    ])
                for f in range(times):
                    even, odd = mixed[0][f], mixed[1][f]
                    for y in range(lines):
                        at = slice(y * NX, (y + 1) * NX)
                        both = jnp.concatenate([even[:, at], odd[:, at]], axis=1)
                        out_ref[:, f, :, pair, y] = both.reshape(grid_size, pw_size, rows, 2 * NX)

    out_shape = (grid_size, times, pw_size, planes // 2, lines, rows, 2 * NX)
    depth = occupied_count + unoccupied_count
    return pl.pallas_call(
        kernel,
        grid=(steps,),
        in_specs=[
            pl.BlockSpec(memory_space=pltpu.SMEM),
            pl.BlockSpec((times, slab, occupied_count), lambda k: (0, 0, 0)),
            pl.BlockSpec((times, slab, DEPTH), lambda k: (0, 0, k)),
            pl.BlockSpec((planes, occupied_count, width), lambda k: (0, 0, 0)),
            pl.BlockSpec((planes, DEPTH, width), lambda k: (0, k, 0)),
        ],
        out_specs=pl.BlockSpec(out_shape, lambda k: (0,) * len(out_shape)),
        out_shape=jax.ShapeDtypeStruct(out_shape, jnp.bfloat16),
        scratch_shapes=[
            pltpu.VMEM((planes, times * slab, width), jnp.float32),
            pltpu.VMEM((planes, times * slab, width), jnp.float32),
        ],
        compiler_params=pltpu.CompilerParams(vmem_limit_bytes=VMEM_LIMIT),
        cost_estimate=expected(2 * times * slab * depth * planes * width, 2 * depth * (times * slab + planes * width)),
        name="respond",
    )(weights, occupied, unoccupied, occupied_planes, unoccupied_planes)


def transform(received, tables, previous, first_pair, total_planes):
    sources, pw_size, pairs, lines, rows, width = received.shape
    number = sources * lines
    line_table, high_table, low_table = tables
    pairs_of_pw = total_planes // (2 * pw_size)
    together = 2
    batch = 8

    def kernel(line_ref, high_ref, low_ref, in_ref, *rest):
        out_ref, sides_ref = rest[-2:]
        images = jnp.swapaxes(in_ref[...].reshape(number, rows, width), 0, 1)
        for first in range(0, rows, together):
            group = range(first, first + together)
            side_by_side = jnp.concatenate([images[r] for r in group], axis=1)
            lined = jnp.dot(line_ref[...], side_by_side, preferred_element_type=jnp.float32)
            for r in group:
                at, lanes = slice(r * number, (r + 1) * number), slice((r - first) * width, (r - first + 1) * width)
                sides_ref[at, :width] = lined[:number, lanes]
                sides_ref[at, width:] = lined[number:, lanes]
        for first in range(0, rows, batch):
            sides = sides_ref[first * number : (first + batch) * number]
            high = sides.astype(jnp.bfloat16)
            low = (sides - high.astype(jnp.float32)).astype(jnp.bfloat16)
            waves = jnp.dot(high, high_ref[...], preferred_element_type=jnp.float32)
            waves += jnp.dot(low, high_ref[...], preferred_element_type=jnp.float32)
            waves += jnp.dot(high, low_ref[...], preferred_element_type=jnp.float32)
            for plane in range(2):
                lanes = slice(plane * width, (plane + 1) * width)
                out_ref[0, first : first + batch, plane] = waves[:, lanes].reshape(batch, number, width)

    out_shape = (1, rows, total_planes, number, width)
    whole = lambda p, j: (0, 0)
    operands = [line_table, high_table, low_table, received]
    in_specs = [
        pl.BlockSpec(line_table.shape, whole),
        pl.BlockSpec(high_table.shape, whole),
        pl.BlockSpec(low_table.shape, whole),
        pl.BlockSpec((sources, 1, 1, lines, rows, width), lambda p, j: (0, p, j, 0, 0, 0)),
    ]
    aliases = {}
    if previous is not None:
        aliases = {len(operands): 0}
        operands.append(previous)
        in_specs.append(pl.BlockSpec(memory_space=pl.ANY))
    work = pw_size * pairs * rows * number
    return pl.pallas_call(
        kernel,
        grid=(pw_size, pairs),
        in_specs=in_specs,
        out_specs=pl.BlockSpec(
            (1, rows, 2, number, width), lambda p, j: (0, 0, p * pairs_of_pw + first_pair + j, 0, 0)
        ),
        out_shape=jax.ShapeDtypeStruct(out_shape, jnp.float32),
        scratch_shapes=[pltpu.VMEM((rows * number, 2 * width), jnp.float32)],
        input_output_aliases=aliases,
        compiler_params=pltpu.CompilerParams(vmem_limit_bytes=VMEM_LIMIT),
        cost_estimate=expected(work * 2 * width * (2 * number + 6 * width), work * width * 10),
        name="transform",
    )(*operands)


def ring_places(number):
    order = list(range(0, number, 2)) + list(range(number - 1, 0, -2))
    onward = [(order[n], order[(n + 1) % number]) for n in range(number)]
    back = [(to, source) for source, to in onward]
    arrivals = np.zeros((number, number), np.int32)
    for n, device in enumerate(order):
        sequence = [n]
        for hop in range(1, number // 2):
            sequence += [n - hop, n + hop]
        sequence.append(n + number // 2)
        arrivals[device] = [order[m % number] for m in sequence]
    return onward, back, arrivals


def gather_weighed(mine, orbital_block, core, decays):
    number = lax.axis_size("grid")
    onward, back, arrivals = ring_places(number)
    places = orbital_block[jnp.asarray(arrivals)[lax.axis_index("grid")]]
    middle = mine.shape[0] // 2

    def pair(rows, start):
        return [(rows, 0, start), (lax.ppermute(rows, "tm", SWAP), 1, start)]

    weighed = weigh([pair(mine, 0)], places[:1], core, decays, None)
    up = down = mine
    for hop in range(1, number // 2):
        up, down = lax.ppermute(up, "grid", onward), lax.ppermute(down, "grid", back)
        blocks = [pair(up, 0), pair(down, 0)]
        weighed = weigh(blocks, places[2 * hop - 1 : 2 * hop + 1], core, decays, weighed)
    up, down = lax.ppermute(up[:middle], "grid", onward), lax.ppermute(down[middle:], "grid", back)
    blocks = [pair(up, 0) + pair(down, middle)]
    return weigh(blocks, places[number - 1 :], core, decays, weighed)


def shards(
    slab_orbitals,
    orbital_block,
    occupied_columns,
    unoccupied_columns,
    occupied_gap,
    unoccupied_gap,
    time_table,
    frequency_table,
    time_weight,
    time_index,
    frequency_index,
):
    grid_size, tm_size, pw_size = (lax.axis_size(axis) for axis in AXES)
    planes_local = occupied_columns.shape[1]
    moment = lax.axis_index("tm").astype(jnp.int32)
    core = moment.reshape(1)
    half = SLAB // tm_size

    rows = jnp.transpose(slab_orbitals[0])
    mine = lax.dynamic_slice_in_dim(rows, moment * half, half, 0)

    time_points = time_table[time_index]
    frequency_weights = time_weight[time_index][None, :] * jnp.cos(
        frequency_table[frequency_index][:, None] * time_points[None, :]
    )
    occupied_decay = jnp.exp(-occupied_gap[None, :] * time_points[:, None])
    unoccupied_decay = jnp.exp(-unoccupied_gap[None, :] * time_points[:, None])

    occupied, unoccupied = gather_weighed(mine, orbital_block, core, (occupied_decay, unoccupied_decay))
    occupied_planes = split_planes(occupied_columns, core, 0, occupied_columns.shape[0] // DEPTH, None)
    unoccupied_planes = None
    steps = unoccupied_columns.shape[0] // DEPTH // SPLIT_CALLS
    for call in range(SPLIT_CALLS):
        unoccupied_planes = split_planes(unoccupied_columns, core, call * steps, steps, unoccupied_planes)

    tables = (jnp.asarray(line_operator(NY)),) + tuple(jnp.asarray(t) for t in row_operator(NX))
    result = None
    first_pair = 0
    for pairs, occupied_part, unoccupied_part in zip(PAIR_CHUNKS, occupied_planes, unoccupied_planes):
        sent = respond(
            -frequency_weights, occupied, unoccupied, occupied_part, unoccupied_part, (grid_size, pw_size)
        )
        sent = sent.reshape((-1,) + sent.shape[3:])
        received = lax.all_to_all(sent, AXES, split_axis=0, concat_axis=0, tiled=True)
        received = received.reshape((grid_size * tm_size, pw_size) + received.shape[1:])
        result = transform(received, tables, result, first_pair, pw_size * planes_local)
        first_pair += pairs
    return result


def solution(mesh):
    placed = (
        P("grid", None, None),
        P(),
        P(None, "pw", "grid"),
        P(None, "pw", "grid"),
        P(),
        P(),
        P(),
        P(),
        P(),
        P(),
        P(),
    )
    rows = SLAB // (mesh.shape["grid"] * mesh.shape["pw"])
    lanes = NX * NY // (mesh.shape["grid"] * mesh.shape["tm"])
    fits = rows % GROUP == 0 and lanes % 128 == 0
    return jax.shard_map(
        shards if fits else general_shards,
        mesh=mesh,
        in_specs=placed,
        out_specs=P("tm", ("grid", "pw"), None, None, None),
        check_vma=False,
    )
```

```python
import math

import jax
import jax.numpy as jnp
import ml_dtypes
import numpy as np
from jax import lax
from jax.experimental import pallas as pl
from jax.experimental.pallas import tpu as pltpu
from jax.sharding import PartitionSpec as P

NX = 64
NY = 64
SLAB = 512


def dft_angles(number):
    indices = jnp.arange(number, dtype=jnp.int32)
    product = indices[:, None] * indices[None, :] % number
    return product.astype(jnp.float32) * (2.0 * math.pi / number)


def row_table(number):
    angles = dft_angles(number)
    factor = 1.0 / math.sqrt(number)
    return jnp.concatenate([jnp.cos(angles), -jnp.sin(angles)], axis=1) * factor


def column_table(number):
    angles = dft_angles(number)
    factor = 1.0 / math.sqrt(number)
    return (jnp.concatenate([jnp.cos(angles), jnp.sin(angles)], axis=0) * factor).astype(
        jnp.bfloat16
    )


def combine_parts(y_parts, width_y, width_x):
    cosine = y_parts[..., :width_y, :]
    sine = y_parts[..., width_y:, :]
    real_part = cosine[..., :width_x] + sine[..., width_x:]
    imag_part = cosine[..., width_x:] - sine[..., :width_x]
    return jnp.concatenate([real_part, imag_part], axis=-1)


def weigh_rows(values, rates, time_point):
    return (values * jnp.exp(-rates * time_point)[:, :, None]).astype(jnp.bfloat16)


def general_shards(
    slab_orbitals,
    orbital_block,
    occupied_columns,
    unoccupied_columns,
    occupied_gap,
    unoccupied_gap,
    time_table,
    frequency_table,
    time_weight,
    time_index,
    frequency_index,
):
    block_count = lax.axis_size("grid")
    occupied_block = occupied_columns.shape[0] // block_count
    unoccupied_block = unoccupied_columns.shape[0] // block_count
    planes_local = occupied_columns.shape[1]
    lines_local = occupied_columns.shape[2] // NX
    width = planes_local * occupied_columns.shape[2]
    occupied_blocks = occupied_columns.reshape(block_count, occupied_block, width)
    unoccupied_blocks = unoccupied_columns.reshape(block_count, unoccupied_block, width)
    occupied_rates = occupied_gap.reshape(block_count, occupied_block)
    unoccupied_rates = unoccupied_gap.reshape(block_count, unoccupied_block)
    moment = lax.axis_index("tm")
    time_slot = time_index[moment]
    time_point = time_table[time_slot]
    frequency_weights = time_weight[time_slot] * jnp.cos(
        frequency_table[frequency_index] * time_point
    )
    pieces = lax.all_gather(slab_orbitals, "grid", axis=0, tiled=True)
    occupied_part = weigh_rows(
        pieces[:, :occupied_block, :], jnp.take(occupied_rates, orbital_block, axis=0), time_point
    )
    unoccupied_part = weigh_rows(
        pieces[:, occupied_block:, :], jnp.take(unoccupied_rates, orbital_block, axis=0), time_point
    )
    green_occupied = jnp.einsum(
        "jis,jic->sc",
        occupied_part,
        jnp.take(occupied_blocks, orbital_block, axis=0),
        preferred_element_type=jnp.float32,
    )
    green_unoccupied = jnp.einsum(
        "jis,jic->sc",
        unoccupied_part,
        jnp.take(unoccupied_blocks, orbital_block, axis=0),
        preferred_element_type=jnp.float32,
    )
    green_occupied, green_unoccupied = (green_occupied, green_unoccupied)
    response = -green_occupied * green_unoccupied
    response = response.reshape(SLAB, planes_local, lines_local, NX)
    tiles = jnp.dot(response, row_table(NX), precision=lax.Precision.HIGHEST).astype(jnp.bfloat16)
    y_table = column_table(NY)
    received = lax.all_to_all(
        tiles[:, None], ("grid", "pw"), split_axis=0, concat_axis=1, tiled=True
    )
    stacked = received[None]
    sources = stacked.reshape(
        stacked.shape[0],
        stacked.shape[1],
        block_count,
        lax.axis_size("pw"),
        planes_local,
        lines_local,
        2 * NX,
    )
    y_parts = jnp.einsum(
        "kgy,trgpzyc->trpzkc",
        y_table.reshape(2 * NY, block_count, lines_local),
        sources,
        preferred_element_type=jnp.float32,
    )
    y_parts = y_parts.reshape(
        y_parts.shape[0], y_parts.shape[1], lax.axis_size("pw") * planes_local, 2 * NY, 2 * NX
    )
    plane_waves = combine_parts(y_parts, NY, NX)
    summed = lax.psum(frequency_weights[:, None, None, None, None] * plane_waves[0][None], "tm")
    return lax.dynamic_slice_in_dim(summed, moment, 1, 0)


PARTS = 2
TURN = 64
GROUP = 16
ABSORB_LIMIT = 32 * 2**20
TRANSFORM_LIMIT = 24 * 2**20
SMALL_LIMIT = 2**20
AXES = ("grid", "tm", "pw")
SWAP = [(0, 1), (1, 0)]
TOKEN = jax.ShapeDtypeStruct((8, 128), jnp.float32)


def host_angles(number):
    indices = np.arange(number)
    return (indices[:, None] * indices[None, :] % number) * (2.0 * math.pi / number)


def line_operator(lines):
    angles = host_angles(lines)
    table = np.concatenate([np.cos(angles), np.sin(angles)]) / math.sqrt(lines)
    return table.astype(np.float32).astype(ml_dtypes.bfloat16)


def row_operator(number):
    angles = host_angles(number)
    cosine, sine = np.cos(angles) / math.sqrt(number), np.sin(angles) / math.sqrt(number)
    one = np.stack([np.concatenate([cosine, -sine], 1), np.concatenate([-sine, -cosine], 1)])
    both = np.einsum("sxc,pq->spxqc", one, np.eye(2)).reshape(4 * number, 4 * number)
    high = both.astype(np.float32).astype(ml_dtypes.bfloat16)
    low = (both - high.astype(np.float64)).astype(np.float32).astype(ml_dtypes.bfloat16)
    return high, low


def expected(flops, read_and_written):
    return pl.CostEstimate(flops=flops, bytes_accessed=read_and_written, transcendentals=0)


def hbm(array):
    return pltpu.with_memory_space_constraint(array, pltpu.HBM)


def take_planes(block_ref, out_ref, first):
    for start in range(0, block_ref.shape[0], TURN):
        at = slice(start, start + TURN)
        out_ref[:, first + start : first + start + TURN] = jnp.swapaxes(block_ref[at], 0, 1)


def mix_response(weight_ref, acc_ref, out_ref):
    _, planes, _, width = acc_ref.shape
    grid_size, times, pw_size, _, lines, rows, _ = out_ref.shape
    points = grid_size * pw_size * rows
    for pair in range(planes // 2):
        mixed = []
        for z in (2 * pair, 2 * pair + 1):
            product = acc_ref[0, z] * acc_ref[1, z]
            first, second = product[:points], product[points:]
            mixed.append([
                (weight_ref[f, 0] * first + weight_ref[f, 1] * second).astype(jnp.bfloat16) for f in range(times)
            ])
        for f in range(times):
            even, odd = mixed[0][f], mixed[1][f]
            for y in range(lines):
                at = slice(y * NX, (y + 1) * NX)
                both = jnp.concatenate([even[:, at], odd[:, at]], axis=1)
                out_ref[:, f, :, pair, y] = both.reshape(grid_size, pw_size, rows, 2 * NX)


def absorb(pieces, part, places, core, decays, columns, acc, finish, last):
    occupied_decay, unoccupied_decay = decays
    occupied_columns, unoccupied_columns = columns
    times, occupied_count = occupied_decay.shape
    unoccupied_count = unoccupied_decay.shape[1]
    planes, lanes = occupied_columns.shape[1], occupied_columns.shape[2] // 2
    flat = [entry for block in pieces for entry in block]
    half, width = flat[0][0].shape
    half //= PARTS
    points = 2 * half
    occupied_block = occupied_count * width // (occupied_count + unoccupied_count)
    unoccupied_block = width - occupied_block
    first_call = acc is None

    def kernel(place_ref, core_ref, occ_ref, unocc_ref, occ_col, unocc_col, *rest):
        refs, rest = rest[: len(flat)], rest[len(flat) :]
        if not first_call:
            rest = rest[1:]
        weight_ref, acc_ref, last_ref, weighed, taken = rest
        take_planes(occ_col, taken, 0)
        take_planes(unocc_col, taken, occupied_block)
        for n, block in enumerate(pieces):
            mine, refs = refs[: len(block)], refs[len(block) :]

            @pl.when(pl.program_id(0) == n)
            def _():
                for ref, (_, other) in zip(mine, block):
                    side = 1 - core_ref[0] if other else core_ref[0]
                    values = ref[...].astype(jnp.float32)
                    for t in range(times):
                        at = pl.ds(pl.multiple_of(t * points + side * half, half), half)
                        for low, high, rates in ((0, occupied_block, occ_ref), (occupied_block, width, unocc_ref)):
                            scaled = values[:, low:high] * rates[t : t + 1, :]
                            weighed[at, low:high] = scaled.astype(jnp.bfloat16)

        if first_call:

            @pl.when(pl.program_id(0) == 0)
            def _():
                acc_ref[...] = jnp.zeros_like(acc_ref)

        for z in range(planes):
            for kind, at in enumerate((slice(0, occupied_block), slice(occupied_block, width))):
                acc_ref[kind, z] += jnp.dot(weighed[:, at], taken[z, at], preferred_element_type=jnp.float32)

        if last:

            @pl.when(pl.program_id(0) == len(pieces) - 1)
            def _():
                mix_response(weight_ref, acc_ref, last_ref)

        else:
            last_ref[...] = jnp.zeros_like(last_ref)

    total = (2, planes, times * points, lanes)
    kept = pl.BlockSpec(memory_space=pltpu.VMEM)
    operands = [places, core, occupied_decay, unoccupied_decay, hbm(occupied_columns), hbm(unoccupied_columns)]
    operands += [entry[0] if part == 0 else hbm(entry[0]) for entry in flat]
    in_specs = [
        pl.BlockSpec((times, occupied_block), lambda n, place, core: (0, place[n])),
        pl.BlockSpec((times, unoccupied_block), lambda n, place, core: (0, place[n])),
        pl.BlockSpec((occupied_block, planes, lanes), lambda n, place, core: (place[n], 0, core[0])),
        pl.BlockSpec((unoccupied_block, planes, lanes), lambda n, place, core: (place[n], 0, core[0])),
    ] + [pl.BlockSpec((half, width), lambda n, place, core: (part, 0)) for entry in flat]
    out_specs, out_shape, aliases = [kept], [pltpu.VMEM(total, jnp.float32)], {}
    if not first_call:
        aliases = {len(operands): 0}
        operands.append(acc)
        in_specs.append(kept)
    weights, (grid_size, pw_size) = finish
    operands.append(weights)
    in_specs.append(pl.BlockSpec(memory_space=pltpu.SMEM))
    if last:
        rows = points // (grid_size * pw_size)
        sent = (grid_size, times, pw_size, planes // 2, lanes // NX, rows, 2 * NX)
        out_specs.append(pl.BlockSpec(sent, lambda n, place, core: (0,) * len(sent)))
        out_shape.append(pltpu.HBM(sent, jnp.bfloat16))
    else:
        out_specs.append(pl.BlockSpec(TOKEN.shape, lambda n, place, core: (0, 0)))
        out_shape.append(pltpu.VMEM(TOKEN.shape, TOKEN.dtype))
    blocks = len(pieces)
    return pl.pallas_call(
        kernel,
        grid_spec=pltpu.PrefetchScalarGridSpec(
            num_scalar_prefetch=2,
            grid=(blocks,),
            in_specs=in_specs,
            out_specs=out_specs,
            scratch_shapes=[
                pltpu.VMEM((times * points, width), jnp.bfloat16),
                pltpu.VMEM((planes, width, lanes), jnp.bfloat16),
            ],
        ),
        out_shape=out_shape,
        input_output_aliases=aliases,
        compiler_params=pltpu.CompilerParams(vmem_limit_bytes=ABSORB_LIMIT),
        cost_estimate=expected(
            blocks * 2 * times * points * width * planes * lanes, blocks * 2 * width * (points + planes * lanes)
        ),
        name="absorb",
    )(*operands)


def transform(received, tables, previous, part, total_rows):
    sources, pw_size, pairs, lines, rows, width = received.shape
    number = sources * lines
    line_table, high_table, low_table = tables
    total_planes = 2 * pw_size * pairs
    together = 2
    batch = 8

    def kernel(line_ref, high_ref, low_ref, in_ref, *rest):
        out_ref, sides_ref = rest[-2:]
        images = jnp.swapaxes(in_ref[...].reshape(number, rows, width), 0, 1)
        for first in range(0, rows, together):
            group = range(first, first + together)
            side_by_side = jnp.concatenate([images[r] for r in group], axis=1)
            lined = jnp.dot(line_ref[...], side_by_side, preferred_element_type=jnp.float32)
            for r in group:
                at, lanes = slice(r * number, (r + 1) * number), slice((r - first) * width, (r - first + 1) * width)
                sides_ref[at, :width] = lined[:number, lanes]
                sides_ref[at, width:] = lined[number:, lanes]
        for first in range(0, rows, batch):
            sides = sides_ref[first * number : (first + batch) * number]
            high = sides.astype(jnp.bfloat16)
            low = (sides - high.astype(jnp.float32)).astype(jnp.bfloat16)
            waves = jnp.dot(high, high_ref[...], preferred_element_type=jnp.float32)
            waves += jnp.dot(low, high_ref[...], preferred_element_type=jnp.float32)
            waves += jnp.dot(high, low_ref[...], preferred_element_type=jnp.float32)
            for plane in range(2):
                lanes = slice(plane * width, (plane + 1) * width)
                out_ref[0, first : first + batch, plane] = waves[:, lanes].reshape(batch, number, width)

    out_shape = (1, total_rows, total_planes, number, width)
    whole = lambda p, j: (0, 0)
    operands = [line_table, high_table, low_table, received]
    in_specs = [
        pl.BlockSpec(line_table.shape, whole),
        pl.BlockSpec(high_table.shape, whole),
        pl.BlockSpec(low_table.shape, whole),
        pl.BlockSpec((sources, 1, 1, lines, rows, width), lambda p, j: (0, p, j, 0, 0, 0)),
    ]
    aliases = {}
    if previous is not None:
        aliases = {len(operands): 0}
        operands.append(previous)
        in_specs.append(pl.BlockSpec(memory_space=pl.ANY))
    work = pw_size * pairs * rows * number
    return pl.pallas_call(
        kernel,
        grid=(pw_size, pairs),
        in_specs=in_specs,
        out_specs=pl.BlockSpec(
            (1, rows, 2, number, width), lambda p, j: (0, part, p * pairs + j, 0, 0)
        ),
        out_shape=jax.ShapeDtypeStruct(out_shape, jnp.float32),
        scratch_shapes=[pltpu.VMEM((rows * number, 2 * width), jnp.float32)],
        input_output_aliases=aliases,
        compiler_params=pltpu.CompilerParams(vmem_limit_bytes=TRANSFORM_LIMIT),
        cost_estimate=expected(work * 2 * width * (2 * number + 6 * width), work * width * 10),
        name="transform",
    )(*operands)


def ring_places(number):
    order = list(range(0, number, 2)) + list(range(number - 1, 0, -2))
    onward = [(order[n], order[(n + 1) % number]) for n in range(number)]
    back = [(to, source) for source, to in onward]
    arrivals = np.zeros((number, number), np.int32)
    for n, device in enumerate(order):
        sequence = [n]
        for hop in range(1, number // 2):
            sequence += [n - hop, n + hop]
        sequence.append(n + number // 2)
        arrivals[device] = [order[m % number] for m in sequence]
    return onward, back, arrivals


def after(arrays, token):
    count = len(arrays)
    anywhere = pl.BlockSpec(memory_space=pl.ANY)
    return pl.pallas_call(
        lambda *refs: None,
        in_specs=[anywhere] * count + [pl.BlockSpec(memory_space=pltpu.VMEM)],
        out_specs=[anywhere] * count,
        out_shape=[jax.ShapeDtypeStruct(array.shape, array.dtype) for array in arrays],
        input_output_aliases={n: n for n in range(count)},
        compiler_params=pltpu.CompilerParams(vmem_limit_bytes=SMALL_LIMIT),
        name="after",
    )(*arrays, pltpu.with_memory_space_constraint(token, pltpu.VMEM))


def choose(core, first, second):
    def kernel(core_ref, first_ref, second_ref, out_ref):
        @pl.when(core_ref[0] == 0)
        def _():
            out_ref[...] = first_ref[...]

        @pl.when(core_ref[0] != 0)
        def _():
            out_ref[...] = second_ref[...]

    kept = pl.BlockSpec(memory_space=pltpu.VMEM)
    return pl.pallas_call(
        kernel,
        in_specs=[pl.BlockSpec(memory_space=pltpu.SMEM), kept, kept],
        out_specs=kept,
        out_shape=pltpu.VMEM(first.shape, first.dtype),
        compiler_params=pltpu.CompilerParams(vmem_limit_bytes=4 * SMALL_LIMIT),
        name="choose",
    )(core, first, second)


def swapped(rows):
    return [(rows, 0), (lax.ppermute(rows, "tm", SWAP), 1)]


def pick(table, index):
    here = index[..., None] == jnp.arange(table.shape[0], dtype=index.dtype)
    return jnp.sum(jnp.where(here, table, jnp.zeros_like(table)), axis=-1)


def gather_and_absorb(mine, core, places, ring, absorb_blocks):
    number = lax.axis_size("grid")
    onward, back = ring
    blocks, every, acc = [swapped(mine)], [], None
    up = down = mine
    for hops in range(1, number // 2):
        up, down = lax.ppermute(up, "grid", onward), lax.ppermute(down, "grid", back)
        start = len(every)
        every += blocks
        acc, token = absorb_blocks(blocks, 0, places[start : len(every)], acc, False)
        up, down = after([up, down], token)
        blocks = [swapped(up), swapped(down)]
    far = choose(core, up, down)
    sides = list(enumerate((onward, back)))
    far = [
        lax.ppermute(far, ("grid", "tm"), [(2 * source + side, 2 * to + (side ^ flip)) for side, pairs in sides for source, to in pairs])
        for flip in (0, 1)
    ]
    start = len(every)
    every += blocks
    acc, token = absorb_blocks(blocks, 0, places[start : len(every)], acc, False)
    own, other = after(far, token)
    blocks = [[(own, 0), (other, 1)]]
    _, sent = absorb_blocks(blocks, 0, places[number - 1 :], acc, True)
    return sent, every + blocks


def shards(
    slab_orbitals,
    orbital_block,
    occupied_columns,
    unoccupied_columns,
    occupied_gap,
    unoccupied_gap,
    time_table,
    frequency_table,
    time_weight,
    time_index,
    frequency_index,
):
    grid_size, tm_size, pw_size = (lax.axis_size(axis) for axis in AXES)
    moment = lax.axis_index("tm").astype(jnp.int32)
    core = moment.reshape(1)
    owners = grid_size * pw_size
    rows = SLAB // owners
    part_rows = rows // PARTS

    by_owner = jnp.transpose(slab_orbitals[0]).reshape(owners, PARTS, part_rows, -1)
    by_owner = lax.dynamic_slice_in_dim(by_owner, moment * (owners // tm_size), owners // tm_size, 0)
    onward, back, arrivals = ring_places(grid_size)
    arrivals = jnp.asarray(arrivals)
    mine_first = jnp.arange(grid_size)[:, None] == lax.axis_index("grid")
    places = pick(orbital_block, jnp.sum(jnp.where(mine_first, arrivals, 0), axis=0))

    time_points = pick(time_table, time_index)
    frequency_weights = pick(time_weight, time_index)[None, :] * jnp.cos(
        pick(frequency_table, frequency_index)[:, None] * time_points[None, :]
    )
    occupied_decay = jnp.exp(-occupied_gap[None, :] * time_points[:, None])
    unoccupied_decay = jnp.exp(-unoccupied_gap[None, :] * time_points[:, None])

    columns = (occupied_columns, unoccupied_columns)
    finish = (-frequency_weights, (grid_size, pw_size))

    def absorb_blocks(pieces, part, here, acc, last):
        return absorb(pieces, part, here, core, (occupied_decay, unoccupied_decay), columns, acc, finish, last)

    tables = (jnp.asarray(line_operator(NY)),) + tuple(jnp.asarray(t) for t in row_operator(NX))
    mine = jnp.swapaxes(by_owner, 0, 1).reshape(SLAB // tm_size, -1)
    result = None
    for part in range(PARTS):
        if part == 0:
            sent, blocks = gather_and_absorb(mine, core, places, (onward, back), absorb_blocks)
        else:
            _, sent = absorb_blocks(blocks, part, places, None, True)
        sent = sent.reshape((-1,) + sent.shape[3:])
        received = lax.all_to_all(sent, AXES, split_axis=0, concat_axis=0, tiled=True)
        received = received.reshape((grid_size * tm_size, pw_size) + received.shape[1:])
        result = transform(received, tables, result, part, rows)
    return result


def solution(mesh):
    placed = (
        P("grid", None, None),
        P(),
        P(None, "pw", "grid"),
        P(None, "pw", "grid"),
        P(),
        P(),
        P(),
        P(),
        P(),
        P(),
        P(),
    )
    rows = SLAB // (mesh.shape["grid"] * mesh.shape["pw"])
    lanes = NX * NY // (mesh.shape["grid"] * mesh.shape["tm"])
    fits = rows % (GROUP * PARTS) == 0 and lanes % 128 == 0
    return jax.shard_map(
        shards if fits else general_shards,
        mesh=mesh,
        in_specs=placed,
        out_specs=P("tm", ("grid", "pw"), None, None, None),
        check_vma=False,
    )
```

```python
import math

import jax
import jax.numpy as jnp
import ml_dtypes
import numpy as np
from jax import lax
from jax.experimental import pallas as pl
from jax.experimental.pallas import tpu as pltpu
from jax.sharding import PartitionSpec as P

NX = 64
NY = 64
SLAB = 512


def dft_angles(number):
    indices = jnp.arange(number, dtype=jnp.int32)
    product = indices[:, None] * indices[None, :] % number
    return product.astype(jnp.float32) * (2.0 * math.pi / number)


def row_table(number):
    angles = dft_angles(number)
    factor = 1.0 / math.sqrt(number)
    return jnp.concatenate([jnp.cos(angles), -jnp.sin(angles)], axis=1) * factor


def column_table(number):
    angles = dft_angles(number)
    factor = 1.0 / math.sqrt(number)
    return (jnp.concatenate([jnp.cos(angles), jnp.sin(angles)], axis=0) * factor).astype(
        jnp.bfloat16
    )


def combine_parts(y_parts, width_y, width_x):
    cosine = y_parts[..., :width_y, :]
    sine = y_parts[..., width_y:, :]
    real_part = cosine[..., :width_x] + sine[..., width_x:]
    imag_part = cosine[..., width_x:] - sine[..., :width_x]
    return jnp.concatenate([real_part, imag_part], axis=-1)


def weigh_rows(values, rates, time_point):
    return (values * jnp.exp(-rates * time_point)[:, :, None]).astype(jnp.bfloat16)


def general_shards(
    slab_orbitals,
    orbital_block,
    occupied_columns,
    unoccupied_columns,
    occupied_gap,
    unoccupied_gap,
    time_table,
    frequency_table,
    time_weight,
    time_index,
    frequency_index,
):
    block_count = lax.axis_size("grid")
    occupied_block = occupied_columns.shape[0] // block_count
    unoccupied_block = unoccupied_columns.shape[0] // block_count
    planes_local = occupied_columns.shape[1]
    lines_local = occupied_columns.shape[2] // NX
    width = planes_local * occupied_columns.shape[2]
    occupied_blocks = occupied_columns.reshape(block_count, occupied_block, width)
    unoccupied_blocks = unoccupied_columns.reshape(block_count, unoccupied_block, width)
    occupied_rates = occupied_gap.reshape(block_count, occupied_block)
    unoccupied_rates = unoccupied_gap.reshape(block_count, unoccupied_block)
    moment = lax.axis_index("tm")
    time_slot = time_index[moment]
    time_point = time_table[time_slot]
    frequency_weights = time_weight[time_slot] * jnp.cos(
        frequency_table[frequency_index] * time_point
    )
    pieces = lax.all_gather(slab_orbitals, "grid", axis=0, tiled=True)
    occupied_part = weigh_rows(
        pieces[:, :occupied_block, :], jnp.take(occupied_rates, orbital_block, axis=0), time_point
    )
    unoccupied_part = weigh_rows(
        pieces[:, occupied_block:, :], jnp.take(unoccupied_rates, orbital_block, axis=0), time_point
    )
    green_occupied = jnp.einsum(
        "jis,jic->sc",
        occupied_part,
        jnp.take(occupied_blocks, orbital_block, axis=0),
        preferred_element_type=jnp.float32,
    )
    green_unoccupied = jnp.einsum(
        "jis,jic->sc",
        unoccupied_part,
        jnp.take(unoccupied_blocks, orbital_block, axis=0),
        preferred_element_type=jnp.float32,
    )
    green_occupied, green_unoccupied = (green_occupied, green_unoccupied)
    response = -green_occupied * green_unoccupied
    response = response.reshape(SLAB, planes_local, lines_local, NX)
    tiles = jnp.dot(response, row_table(NX), precision=lax.Precision.HIGHEST).astype(jnp.bfloat16)
    y_table = column_table(NY)
    received = lax.all_to_all(
        tiles[:, None], ("grid", "pw"), split_axis=0, concat_axis=1, tiled=True
    )
    stacked = received[None]
    sources = stacked.reshape(
        stacked.shape[0],
        stacked.shape[1],
        block_count,
        lax.axis_size("pw"),
        planes_local,
        lines_local,
        2 * NX,
    )
    y_parts = jnp.einsum(
        "kgy,trgpzyc->trpzkc",
        y_table.reshape(2 * NY, block_count, lines_local),
        sources,
        preferred_element_type=jnp.float32,
    )
    y_parts = y_parts.reshape(
        y_parts.shape[0], y_parts.shape[1], lax.axis_size("pw") * planes_local, 2 * NY, 2 * NX
    )
    plane_waves = combine_parts(y_parts, NY, NX)
    summed = lax.psum(frequency_weights[:, None, None, None, None] * plane_waves[0][None], "tm")
    return lax.dynamic_slice_in_dim(summed, moment, 1, 0)


PARTS = 2
EXCHANGES = ((0, 0, 4), (1, 0, 4))
TURN = 64
GROUP = 16
ABSORB_LIMIT = 32 * 2**20
TRANSFORM_LIMIT = 24 * 2**20
SMALL_LIMIT = 2**20
AXES = ("grid", "tm", "pw")
SWAP = [(0, 1), (1, 0)]
TOKEN = jax.ShapeDtypeStruct((8, 128), jnp.float32)


def host_angles(number):
    indices = np.arange(number)
    return (indices[:, None] * indices[None, :] % number) * (2.0 * math.pi / number)


def line_operator(lines):
    angles = host_angles(lines)
    table = np.concatenate([np.cos(angles), np.sin(angles)]) / math.sqrt(lines)
    return table.astype(np.float32).astype(ml_dtypes.bfloat16)


def row_operator(number):
    angles = host_angles(number)
    cosine, sine = np.cos(angles) / math.sqrt(number), np.sin(angles) / math.sqrt(number)
    one = np.stack([np.concatenate([cosine, -sine], 1), np.concatenate([-sine, -cosine], 1)])
    both = np.einsum("sxc,pq->spxqc", one, np.eye(2)).reshape(4 * number, 4 * number)
    high = both.astype(np.float32).astype(ml_dtypes.bfloat16)
    low = (both - high.astype(np.float64)).astype(np.float32).astype(ml_dtypes.bfloat16)
    return high, low


def expected(flops, read_and_written):
    return pl.CostEstimate(flops=flops, bytes_accessed=read_and_written, transcendentals=0)


def hbm(array):
    return pltpu.with_memory_space_constraint(array, pltpu.HBM)


def take_planes(block_ref, out_ref, row, first):
    planes = out_ref.shape[0]
    for start in range(0, block_ref.shape[0], TURN):
        turned = jnp.swapaxes(block_ref[start : start + TURN], 0, 1)
        out_ref[:, row + start : row + start + TURN] = turned[first : first + planes]


def mix_response(weight_ref, acc_ref, out_ref):
    _, planes, _, width = acc_ref.shape
    grid_size, times, pw_size, _, lines, rows, _ = out_ref.shape
    points = grid_size * pw_size * rows
    for pair in range(planes // 2):
        mixed = []
        for z in (2 * pair, 2 * pair + 1):
            product = acc_ref[0, z] * acc_ref[1, z]
            first, second = product[:points], product[points:]
            mixed.append([
                (weight_ref[f, 0] * first + weight_ref[f, 1] * second).astype(jnp.bfloat16) for f in range(times)
            ])
        for f in range(times):
            even, odd = mixed[0][f], mixed[1][f]
            for y in range(lines):
                at = slice(y * NX, (y + 1) * NX)
                both = jnp.concatenate([even[:, at], odd[:, at]], axis=1)
                out_ref[:, f, :, pair, y] = both.reshape(grid_size, pw_size, rows, 2 * NX)


def absorb(pieces, exchange, places, core, decays, columns, acc, finish, last):
    occupied_decay, unoccupied_decay = decays
    occupied_columns, unoccupied_columns = columns
    times, occupied_count = occupied_decay.shape
    unoccupied_count = unoccupied_decay.shape[1]
    part, first_pair, pairs = exchange
    planes, planes_local, lanes = 2 * pairs, occupied_columns.shape[1], occupied_columns.shape[2] // 2
    flat = [entry for block in pieces for entry in block]
    width = flat[0][0].shape[1]
    half = SLAB // 2 // PARTS
    points = 2 * half
    occupied_block = occupied_count * width // (occupied_count + unoccupied_count)
    unoccupied_block = width - occupied_block
    first_call = acc is None

    def kernel(place_ref, core_ref, occ_ref, unocc_ref, occ_col, unocc_col, *rest):
        refs, rest = rest[: len(flat)], rest[len(flat) :]
        if not first_call:
            rest = rest[1:]
        weight_ref, acc_ref, last_ref, weighed, taken = rest
        take_planes(occ_col, taken, 0, 2 * first_pair)
        take_planes(unocc_col, taken, occupied_block, 2 * first_pair)
        for n, block in enumerate(pieces):
            mine, refs = refs[: len(block)], refs[len(block) :]

            @pl.when(pl.program_id(0) == n)
            def _():
                for ref, (_, other) in zip(mine, block):
                    side = 1 - core_ref[0] if other else core_ref[0]
                    values = ref[...].astype(jnp.float32)
                    for t in range(times):
                        at = pl.ds(pl.multiple_of(t * points + side * half, half), half)
                        for low, high, rates in ((0, occupied_block, occ_ref), (occupied_block, width, unocc_ref)):
                            scaled = values[:, low:high] * rates[t : t + 1, :]
                            weighed[at, low:high] = scaled.astype(jnp.bfloat16)

        if first_call:

            @pl.when(pl.program_id(0) == 0)
            def _():
                acc_ref[...] = jnp.zeros_like(acc_ref)

        for z in range(planes):
            for kind, at in enumerate((slice(0, occupied_block), slice(occupied_block, width))):
                acc_ref[kind, z] += jnp.dot(weighed[:, at], taken[z, at], preferred_element_type=jnp.float32)

        if last:

            @pl.when(pl.program_id(0) == len(pieces) - 1)
            def _():
                mix_response(weight_ref, acc_ref, last_ref)

        else:
            last_ref[...] = jnp.zeros_like(last_ref)

    total = (2, planes, times * points, lanes)
    kept = pl.BlockSpec(memory_space=pltpu.VMEM)
    operands = [places, core, occupied_decay, unoccupied_decay, hbm(occupied_columns), hbm(unoccupied_columns)]
    operands += [hbm(entry[0]) if first_call and last else entry[0] for entry in flat]
    in_specs = [
        pl.BlockSpec((times, occupied_block), lambda n, place, core: (0, place[n])),
        pl.BlockSpec((times, unoccupied_block), lambda n, place, core: (0, place[n])),
        pl.BlockSpec((occupied_block, planes_local, lanes), lambda n, place, core: (place[n], 0, core[0])),
        pl.BlockSpec((unoccupied_block, planes_local, lanes), lambda n, place, core: (place[n], 0, core[0])),
    ] + [pl.BlockSpec((half, width), lambda n, place, core: (part, 0)) for entry in flat]
    out_specs, out_shape, aliases = [kept], [pltpu.VMEM(total, jnp.float32)], {}
    if not first_call:
        aliases = {len(operands): 0}
        operands.append(acc)
        in_specs.append(kept)
    weights, (grid_size, pw_size) = finish
    operands.append(weights)
    in_specs.append(pl.BlockSpec(memory_space=pltpu.SMEM))
    if last:
        rows = points // (grid_size * pw_size)
        sent = (grid_size, times, pw_size, planes // 2, lanes // NX, rows, 2 * NX)
        out_specs.append(pl.BlockSpec(sent, lambda n, place, core: (0,) * len(sent)))
        out_shape.append(pltpu.HBM(sent, jnp.bfloat16))
    else:
        out_specs.append(pl.BlockSpec(TOKEN.shape, lambda n, place, core: (0, 0)))
        out_shape.append(pltpu.VMEM(TOKEN.shape, TOKEN.dtype))
    blocks = len(pieces)
    return pl.pallas_call(
        kernel,
        grid_spec=pltpu.PrefetchScalarGridSpec(
            num_scalar_prefetch=2,
            grid=(blocks,),
            in_specs=in_specs,
            out_specs=out_specs,
            scratch_shapes=[
                pltpu.VMEM((times * points, width), jnp.bfloat16),
                pltpu.VMEM((planes, width, lanes), jnp.bfloat16),
            ],
        ),
        out_shape=out_shape,
        input_output_aliases=aliases,
        compiler_params=pltpu.CompilerParams(vmem_limit_bytes=ABSORB_LIMIT),
        cost_estimate=expected(
            blocks * 2 * times * points * width * planes * lanes, blocks * 2 * width * (points + planes_local * lanes)
        ),
        name="absorb",
    )(*operands)


def transform(received, tables, previous, exchange, total_rows, total_pairs):
    sources, pw_size, pairs, lines, rows, width = received.shape
    number = sources * lines
    line_table, high_table, low_table = tables
    part, first_pair, _ = exchange
    step = 2 if first_pair % 2 == 0 and pairs % 2 == 0 and total_pairs % 2 == 0 else 1
    together = 2

    def kernel(line_ref, high_ref, low_ref, in_ref, *rest):
        out_ref, sides_ref = rest[-2:]
        for pair in range(step):
            images = jnp.swapaxes(in_ref[:, 0, pair].reshape(number, rows, width), 0, 1)
            for first in range(0, rows, together):
                group = range(first, first + together)
                side_by_side = jnp.concatenate([images[r] for r in group], axis=1)
                lined = jnp.dot(line_ref[...], side_by_side, preferred_element_type=jnp.float32)
                for r in group:
                    at, lanes = slice(r * number, (r + 1) * number), slice((r - first) * width, (r - first + 1) * width)
                    sides_ref[at, :width] = lined[:number, lanes]
                    sides_ref[at, width:] = lined[number:, lanes]
            sides = sides_ref[...]
            high = sides.astype(jnp.bfloat16)
            low = (sides - high.astype(jnp.float32)).astype(jnp.bfloat16)
            waves = jnp.dot(high, high_ref[...], preferred_element_type=jnp.float32)
            waves += jnp.dot(low, high_ref[...], preferred_element_type=jnp.float32)
            waves += jnp.dot(high, low_ref[...], preferred_element_type=jnp.float32)
            for plane in range(2):
                lanes = slice(plane * width, (plane + 1) * width)
                out_ref[0, :, 2 * pair + plane] = waves[:, lanes].reshape(rows, number, width)

    out_shape = (1, total_rows, 2 * pw_size * total_pairs, number, width)
    whole = lambda p, j: (0, 0)
    operands = [line_table, high_table, low_table, received]
    in_specs = [
        pl.BlockSpec(line_table.shape, whole),
        pl.BlockSpec(high_table.shape, whole),
        pl.BlockSpec(low_table.shape, whole),
        pl.BlockSpec((sources, 1, step, lines, rows, width), lambda p, j: (0, p, j, 0, 0, 0)),
    ]
    aliases = {}
    if previous is not None:
        aliases = {len(operands): 0}
        operands.append(previous)
        in_specs.append(pl.BlockSpec(memory_space=pl.ANY))
    work = pw_size * pairs * rows * number
    return pl.pallas_call(
        kernel,
        grid=(pw_size, pairs // step),
        in_specs=in_specs,
        out_specs=pl.BlockSpec(
            (1, rows, 2 * step, number, width), lambda p, j: (0, part, (p * total_pairs + first_pair) // step + j, 0, 0)
        ),
        out_shape=jax.ShapeDtypeStruct(out_shape, jnp.float32),
        scratch_shapes=[pltpu.VMEM((rows * number, 2 * width), jnp.float32)],
        input_output_aliases=aliases,
        compiler_params=pltpu.CompilerParams(vmem_limit_bytes=TRANSFORM_LIMIT),
        cost_estimate=expected(work * 2 * width * (2 * number + 6 * width), work * width * 10),
        name="transform",
    )(*operands)


def ring_places(number):
    order = list(range(0, number, 2)) + list(range(number - 1, 0, -2))
    onward = [(order[n], order[(n + 1) % number]) for n in range(number)]
    back = [(to, source) for source, to in onward]
    arrivals = np.zeros((number, number), np.int32)
    for n, device in enumerate(order):
        sequence = [n]
        for hop in range(1, number // 2):
            sequence += [n - hop, n + hop]
        sequence.append(n + number // 2)
        arrivals[device] = [order[m % number] for m in sequence]
    return onward, back, arrivals


def after(arrays, token):
    count = len(arrays)
    anywhere = pl.BlockSpec(memory_space=pl.ANY)
    return pl.pallas_call(
        lambda *refs: None,
        in_specs=[anywhere] * count + [pl.BlockSpec(memory_space=pltpu.VMEM)],
        out_specs=[anywhere] * count,
        out_shape=[jax.ShapeDtypeStruct(array.shape, array.dtype) for array in arrays],
        input_output_aliases={n: n for n in range(count)},
        compiler_params=pltpu.CompilerParams(vmem_limit_bytes=SMALL_LIMIT),
        name="after",
    )(*arrays, pltpu.with_memory_space_constraint(token, pltpu.VMEM))


def choose(core, first, second):
    shape, dtype = first.shape, first.dtype
    some = (shape[0] // PARTS, shape[1])

    def kernel(core_ref, first_ref, second_ref, out_ref, some_ref):
        for core_index, ref in enumerate((first_ref, second_ref)):

            @pl.when(core_ref[0] == core_index)
            def _():
                out_ref[...] = ref[...]
                some_ref[...] = ref[: some[0]]

    kept = pl.BlockSpec(memory_space=pltpu.VMEM)
    return pl.pallas_call(
        kernel,
        in_specs=[pl.BlockSpec(memory_space=pltpu.SMEM), kept, kept],
        out_specs=[kept, kept],
        out_shape=[pltpu.VMEM(shape, dtype), pltpu.VMEM(some, dtype)],
        compiler_params=pltpu.CompilerParams(vmem_limit_bytes=4 * SMALL_LIMIT),
        name="choose",
    )(core, first, second)


def swapped(rows):
    return [(rows, 0), (lax.ppermute(rows, "tm", SWAP), 1)]


def pick(table, index):
    here = index[..., None] == jnp.arange(table.shape[0], dtype=index.dtype)
    return jnp.sum(jnp.where(here, table, jnp.zeros_like(table)), axis=-1)


def gather_and_absorb(mine, core, places, ring, absorb_blocks):
    number = lax.axis_size("grid")
    onward, back = ring
    blocks, every, acc = [swapped(mine)], [], None
    up = down = mine
    for hops in range(1, number // 2):
        up, down = lax.ppermute(up, "grid", onward), lax.ppermute(down, "grid", back)
        start = len(every)
        every += blocks
        acc, token = absorb_blocks(blocks, EXCHANGES[0], places[start : len(every)], acc, False)
        up, down = after([up, down], token)
        blocks = [swapped(up), swapped(down)]
    far, some = choose(core, up, down)
    sides = list(enumerate((onward, back)))
    own, other = [
        lax.ppermute(
            rows, ("grid", "tm"), [(2 * source + side, 2 * to + (side ^ flip)) for side, pairs in sides for source, to in pairs]
        )
        for rows, flip in ((far, 0), (some, 1))
    ]
    start = len(every)
    every += blocks
    acc, token = absorb_blocks(blocks, EXCHANGES[0], places[start : len(every)], acc, False)
    own, other = after([own, other], token)
    blocks = [[(own, 0), (other, 1)]]
    _, sent = absorb_blocks(blocks, EXCHANGES[0], places[number - 1 :], acc, True)
    return sent, every + blocks, every + [swapped(own)]


def shards(
    slab_orbitals,
    orbital_block,
    occupied_columns,
    unoccupied_columns,
    occupied_gap,
    unoccupied_gap,
    time_table,
    frequency_table,
    time_weight,
    time_index,
    frequency_index,
):
    grid_size, tm_size, pw_size = (lax.axis_size(axis) for axis in AXES)
    moment = lax.axis_index("tm").astype(jnp.int32)
    core = moment.reshape(1)
    owners = grid_size * pw_size
    rows = SLAB // owners
    part_rows = rows // PARTS

    by_owner = jnp.transpose(slab_orbitals[0]).reshape(owners, PARTS, part_rows, -1)
    by_owner = lax.dynamic_slice_in_dim(by_owner, moment * (owners // tm_size), owners // tm_size, 0)
    onward, back, arrivals = ring_places(grid_size)
    arrivals = jnp.asarray(arrivals)
    mine_first = jnp.arange(grid_size)[:, None] == lax.axis_index("grid")
    places = pick(orbital_block, jnp.sum(jnp.where(mine_first, arrivals, 0), axis=0))

    time_points = pick(time_table, time_index)
    frequency_weights = pick(time_weight, time_index)[None, :] * jnp.cos(
        pick(frequency_table, frequency_index)[:, None] * time_points[None, :]
    )
    occupied_decay = jnp.exp(-occupied_gap[None, :] * time_points[:, None])
    unoccupied_decay = jnp.exp(-unoccupied_gap[None, :] * time_points[:, None])

    columns = (occupied_columns, unoccupied_columns)
    finish = (-frequency_weights, (grid_size, pw_size))

    def absorb_blocks(pieces, exchange, here, acc, last):
        return absorb(pieces, exchange, here, core, (occupied_decay, unoccupied_decay), columns, acc, finish, last)

    tables = (jnp.asarray(line_operator(NY)),) + tuple(jnp.asarray(t) for t in row_operator(NX))
    mine = jnp.swapaxes(by_owner, 0, 1).reshape(SLAB // tm_size, -1)
    result = None
    for exchange in EXCHANGES:
        if exchange == EXCHANGES[0]:
            sent, *blocks = gather_and_absorb(mine, core, places, (onward, back), absorb_blocks)
        else:
            _, sent = absorb_blocks(blocks[exchange[0]], exchange, places, None, True)
        sent = sent.reshape((-1,) + sent.shape[3:])
        received = lax.all_to_all(sent, AXES, split_axis=0, concat_axis=0, tiled=True)
        received = received.reshape((grid_size * tm_size, pw_size) + received.shape[1:])
        result = transform(received, tables, result, exchange, rows, occupied_columns.shape[1] // 2)
    return result


def solution(mesh):
    placed = (
        P("grid", None, None),
        P(),
        P(None, "pw", "grid"),
        P(None, "pw", "grid"),
        P(),
        P(),
        P(),
        P(),
        P(),
        P(),
        P(),
    )
    rows = SLAB // (mesh.shape["grid"] * mesh.shape["pw"])
    lanes = NX * NY // (mesh.shape["grid"] * mesh.shape["tm"])
    fits = rows % (GROUP * PARTS) == 0 and lanes % 128 == 0
    return jax.shard_map(
        shards if fits else general_shards,
        mesh=mesh,
        in_specs=placed,
        out_specs=P("tm", ("grid", "pw"), None, None, None),
        check_vma=False,
    )
```

```python
import math

import jax
import jax.numpy as jnp
import ml_dtypes
import numpy as np
from jax import lax
from jax.experimental import pallas as pl
from jax.experimental.pallas import tpu as pltpu
from jax.sharding import PartitionSpec as P

NX = 64
NY = 64
SLAB = 512


def dft_angles(number):
    indices = jnp.arange(number, dtype=jnp.int32)
    product = indices[:, None] * indices[None, :] % number
    return product.astype(jnp.float32) * (2.0 * math.pi / number)


def row_table(number):
    angles = dft_angles(number)
    factor = 1.0 / math.sqrt(number)
    return jnp.concatenate([jnp.cos(angles), -jnp.sin(angles)], axis=1) * factor


def column_table(number):
    angles = dft_angles(number)
    factor = 1.0 / math.sqrt(number)
    return (jnp.concatenate([jnp.cos(angles), jnp.sin(angles)], axis=0) * factor).astype(
        jnp.bfloat16
    )


def combine_parts(y_parts, width_y, width_x):
    cosine = y_parts[..., :width_y, :]
    sine = y_parts[..., width_y:, :]
    real_part = cosine[..., :width_x] + sine[..., width_x:]
    imag_part = cosine[..., width_x:] - sine[..., :width_x]
    return jnp.concatenate([real_part, imag_part], axis=-1)


def weigh_rows(values, rates, time_point):
    return (values * jnp.exp(-rates * time_point)[:, :, None]).astype(jnp.bfloat16)


def general_shards(
    slab_orbitals,
    orbital_block,
    occupied_columns,
    unoccupied_columns,
    occupied_gap,
    unoccupied_gap,
    time_table,
    frequency_table,
    time_weight,
    time_index,
    frequency_index,
):
    block_count = lax.axis_size("grid")
    occupied_block = occupied_columns.shape[0] // block_count
    unoccupied_block = unoccupied_columns.shape[0] // block_count
    planes_local = occupied_columns.shape[1]
    lines_local = occupied_columns.shape[2] // NX
    width = planes_local * occupied_columns.shape[2]
    occupied_blocks = occupied_columns.reshape(block_count, occupied_block, width)
    unoccupied_blocks = unoccupied_columns.reshape(block_count, unoccupied_block, width)
    occupied_rates = occupied_gap.reshape(block_count, occupied_block)
    unoccupied_rates = unoccupied_gap.reshape(block_count, unoccupied_block)
    moment = lax.axis_index("tm")
    time_slot = time_index[moment]
    time_point = time_table[time_slot]
    frequency_weights = time_weight[time_slot] * jnp.cos(
        frequency_table[frequency_index] * time_point
    )
    pieces = lax.all_gather(slab_orbitals, "grid", axis=0, tiled=True)
    occupied_part = weigh_rows(
        pieces[:, :occupied_block, :], jnp.take(occupied_rates, orbital_block, axis=0), time_point
    )
    unoccupied_part = weigh_rows(
        pieces[:, occupied_block:, :], jnp.take(unoccupied_rates, orbital_block, axis=0), time_point
    )
    green_occupied = jnp.einsum(
        "jis,jic->sc",
        occupied_part,
        jnp.take(occupied_blocks, orbital_block, axis=0),
        preferred_element_type=jnp.float32,
    )
    green_unoccupied = jnp.einsum(
        "jis,jic->sc",
        unoccupied_part,
        jnp.take(unoccupied_blocks, orbital_block, axis=0),
        preferred_element_type=jnp.float32,
    )
    green_occupied, green_unoccupied = (green_occupied, green_unoccupied)
    response = -green_occupied * green_unoccupied
    response = response.reshape(SLAB, planes_local, lines_local, NX)
    tiles = jnp.dot(response, row_table(NX), precision=lax.Precision.HIGHEST).astype(jnp.bfloat16)
    y_table = column_table(NY)
    received = lax.all_to_all(
        tiles[:, None], ("grid", "pw"), split_axis=0, concat_axis=1, tiled=True
    )
    stacked = received[None]
    sources = stacked.reshape(
        stacked.shape[0],
        stacked.shape[1],
        block_count,
        lax.axis_size("pw"),
        planes_local,
        lines_local,
        2 * NX,
    )
    y_parts = jnp.einsum(
        "kgy,trgpzyc->trpzkc",
        y_table.reshape(2 * NY, block_count, lines_local),
        sources,
        preferred_element_type=jnp.float32,
    )
    y_parts = y_parts.reshape(
        y_parts.shape[0], y_parts.shape[1], lax.axis_size("pw") * planes_local, 2 * NY, 2 * NX
    )
    plane_waves = combine_parts(y_parts, NY, NX)
    summed = lax.psum(frequency_weights[:, None, None, None, None] * plane_waves[0][None], "tm")
    return lax.dynamic_slice_in_dim(summed, moment, 1, 0)


PARTS = 2
EXCHANGES = ((0, 0, 4), (1, 0, 4))
AHEAD = 1
TURN = 64
GROUP = 16
ABSORB_LIMIT = 16 * 2**20
WHOLE_LIMIT = 28 * 2**20
TRANSFORM_LIMIT = 24 * 2**20
SMALL_LIMIT = 2**20
AXES = ("grid", "tm", "pw")
SWAP = [(0, 1), (1, 0)]
TOKEN = jax.ShapeDtypeStruct((8, 128), jnp.float32)


def host_angles(number):
    indices = np.arange(number)
    return (indices[:, None] * indices[None, :] % number) * (2.0 * math.pi / number)


def line_operator(lines):
    angles = host_angles(lines)
    table = np.concatenate([np.cos(angles), np.sin(angles)]) / math.sqrt(lines)
    return table.astype(np.float32).astype(ml_dtypes.bfloat16)


def row_operator(number):
    angles = host_angles(number)
    cosine, sine = np.cos(angles) / math.sqrt(number), np.sin(angles) / math.sqrt(number)
    one = np.stack([np.concatenate([cosine, -sine], 1), np.concatenate([-sine, -cosine], 1)])
    both = np.einsum("sxc,pq->spxqc", one, np.eye(2)).reshape(4 * number, 4 * number)
    high = both.astype(np.float32).astype(ml_dtypes.bfloat16)
    low = (both - high.astype(np.float64)).astype(np.float32).astype(ml_dtypes.bfloat16)
    return high, low


def expected(flops, read_and_written):
    return pl.CostEstimate(flops=flops, bytes_accessed=read_and_written, transcendentals=0)


def hbm(array):
    return pltpu.with_memory_space_constraint(array, pltpu.HBM)


def take_planes(block_ref, out_ref, row, first):
    planes = out_ref.shape[0]
    for start in range(0, block_ref.shape[0], TURN):
        turned = jnp.swapaxes(block_ref[start : start + TURN], 0, 1)
        out_ref[:, row + start : row + start + TURN] = turned[first : first + planes]


def column_specs(columns, blocks, start):
    return [
        pl.BlockSpec(
            (array.shape[0] // blocks, array.shape[1], array.shape[2] // 2), lambda n, place, core: (place[start + n], 0, core[0])
        )
        for array in columns
    ]


def prepare(places, start, core, small, columns, exchange):
    _, first_pair, pairs = exchange
    blocks = places.shape[0]
    count = blocks - start
    occupied_block = columns[0].shape[0] // blocks
    width = occupied_block + columns[1].shape[0] // blocks
    shape = (count, 2 * pairs, width, columns[0].shape[2] // 2)

    def kernel(place_ref, core_ref, *refs):
        occ_col, unocc_col, ready_ref, token_ref = refs[len(small) :]
        here = ready_ref.at[pl.program_id(0)]
        take_planes(occ_col, here, 0, 2 * first_pair)
        take_planes(unocc_col, here, occupied_block, 2 * first_pair)
        token_ref[...] = jnp.zeros_like(token_ref)

    return pl.pallas_call(
        kernel,
        grid_spec=pltpu.PrefetchScalarGridSpec(
            num_scalar_prefetch=2,
            grid=(count,),
            in_specs=[pl.BlockSpec(memory_space=pltpu.SMEM)] * len(small) + column_specs(columns, blocks, start),
            out_specs=[pl.BlockSpec(memory_space=pltpu.VMEM), pl.BlockSpec(TOKEN.shape, lambda n, place, core: (0, 0))],
        ),
        out_shape=[pltpu.VMEM(shape, jnp.bfloat16), pltpu.VMEM(TOKEN.shape, TOKEN.dtype)],
        compiler_params=pltpu.CompilerParams(vmem_limit_bytes=16 * SMALL_LIMIT),
        cost_estimate=expected(0, 2 * math.prod(shape)),
        name="prepare",
    )(places, core, *small, *[hbm(array) for array in columns])


def mix_response(weight_ref, acc_ref, out_ref):
    _, planes, _, width = acc_ref.shape
    grid_size, times, pw_size, _, lines, rows, _ = out_ref.shape
    points = grid_size * pw_size * rows
    for pair in range(planes // 2):
        mixed = []
        for z in (2 * pair, 2 * pair + 1):
            product = acc_ref[0, z] * acc_ref[1, z]
            first, second = product[:points], product[points:]
            mixed.append([
                (weight_ref[f, 0] * first + weight_ref[f, 1] * second).astype(jnp.bfloat16) for f in range(times)
            ])
        for f in range(times):
            even, odd = mixed[0][f], mixed[1][f]
            for y in range(lines):
                at = slice(y * NX, (y + 1) * NX)
                both = jnp.concatenate([even[:, at], odd[:, at]], axis=1)
                out_ref[:, f, :, pair, y] = both.reshape(grid_size, pw_size, rows, 2 * NX)


def absorb(pieces, exchange, places, start, core, decays, columns, ready, acc, finish, last):
    time_points, occupied_gap, unoccupied_gap = decays
    occupied_columns, unoccupied_columns = columns
    times, occupied_count = time_points.shape[0], occupied_gap.shape[0]
    unoccupied_count = unoccupied_gap.shape[0]
    part, first_pair, pairs = exchange
    planes, planes_local, lanes = 2 * pairs, occupied_columns.shape[1], occupied_columns.shape[2] // 2
    flat = [entry for block in pieces for entry in block]
    width = flat[0][0].shape[1]
    half = SLAB // 2 // PARTS
    points = 2 * half
    occupied_block = occupied_count * width // (occupied_count + unoccupied_count)
    unoccupied_block = width - occupied_block
    first_call = acc is None
    blocks = len(pieces)

    def kernel(place_ref, core_ref, time_ref, occ_ref, unocc_ref, *rest):
        col_refs, rest = rest[: 2 if ready is None else 1], rest[2 if ready is None else 1 :]
        refs, rest = rest[: len(flat)], rest[len(flat) :]
        if not first_call:
            rest = rest[1:]
        weight_ref, acc_ref, last_ref, weighed, *taken = rest
        if ready is None:
            (taken,) = taken
            take_planes(col_refs[0], taken, 0, 2 * first_pair)
            take_planes(col_refs[1], taken, occupied_block, 2 * first_pair)
        else:
            taken = col_refs[0].at[ready[1] + pl.program_id(0)]
        factors = [
            [jnp.exp(-ref[...] * time_ref[t]) for ref in (occ_ref, unocc_ref)] for t in range(times)
        ]
        for n, block in enumerate(pieces):
            mine, refs = refs[: len(block)], refs[len(block) :]

            @pl.when(pl.program_id(0) == n)
            def _():
                for ref, (_, other) in zip(mine, block):
                    side = 1 - core_ref[0] if other else core_ref[0]
                    values = ref[...].astype(jnp.float32)
                    for t in range(times):
                        at = pl.ds(pl.multiple_of(t * points + side * half, half), half)
                        for low, high, factor in ((0, occupied_block, factors[t][0]), (occupied_block, width, factors[t][1])):
                            weighed[at, low:high] = (values[:, low:high] * factor).astype(jnp.bfloat16)

        if first_call and blocks > 1:

            @pl.when(pl.program_id(0) == 0)
            def _():
                acc_ref[...] = jnp.zeros_like(acc_ref)

        for z in range(planes):
            for kind, at in enumerate((slice(0, occupied_block), slice(occupied_block, width))):
                part_sum = jnp.dot(weighed[:, at], taken[z, at], preferred_element_type=jnp.float32)
                if first_call and blocks == 1:
                    acc_ref[kind, z] = part_sum
                else:
                    acc_ref[kind, z] += part_sum

        if last:

            @pl.when(pl.program_id(0) == len(pieces) - 1)
            def _():
                mix_response(weight_ref, acc_ref, last_ref)

        else:
            last_ref[...] = jnp.zeros_like(last_ref)

    total = (2, planes, times * points, lanes)
    kept = pl.BlockSpec(memory_space=pltpu.VMEM)
    operands = [places, core, time_points, occupied_gap.reshape(1, -1), unoccupied_gap.reshape(1, -1)]
    if ready is None:
        operands += [hbm(occupied_columns), hbm(unoccupied_columns)]
        column_in = column_specs(columns, places.shape[0], start)
    else:
        operands.append(pltpu.with_memory_space_constraint(ready[0], pltpu.VMEM))
        column_in = [kept]
    operands += [hbm(entry[0]) if first_call and last else entry[0] for entry in flat]
    in_specs = [
        pl.BlockSpec(memory_space=pltpu.SMEM),
        pl.BlockSpec((1, occupied_block), lambda n, place, core: (0, place[start + n])),
        pl.BlockSpec((1, unoccupied_block), lambda n, place, core: (0, place[start + n])),
        *column_in,
    ] + [pl.BlockSpec((half, width), lambda n, place, core: (part, 0)) for entry in flat]
    out_specs, out_shape, aliases = [kept], [pltpu.VMEM(total, jnp.float32)], {}
    if not first_call:
        aliases = {len(operands): 0}
        operands.append(acc)
        in_specs.append(kept)
    weights, (grid_size, pw_size) = finish
    operands.append(weights)
    in_specs.append(pl.BlockSpec(memory_space=pltpu.SMEM))
    if last:
        rows = points // (grid_size * pw_size)
        sent = (grid_size, times, pw_size, planes // 2, lanes // NX, rows, 2 * NX)
        out_specs.append(pl.BlockSpec(sent, lambda n, place, core: (0,) * len(sent)))
        out_shape.append(pltpu.HBM(sent, jnp.bfloat16))
    else:
        out_specs.append(pl.BlockSpec(TOKEN.shape, lambda n, place, core: (0, 0)))
        out_shape.append(pltpu.VMEM(TOKEN.shape, TOKEN.dtype))
    return pl.pallas_call(
        kernel,
        grid_spec=pltpu.PrefetchScalarGridSpec(
            num_scalar_prefetch=2,
            grid=(blocks,),
            in_specs=in_specs,
            out_specs=out_specs,
            scratch_shapes=[
                pltpu.VMEM((times * points, width), jnp.bfloat16),
            ]
            + ([pltpu.VMEM((planes, width, lanes), jnp.bfloat16)] if ready is None else []),
        ),
        out_shape=out_shape,
        input_output_aliases=aliases,
        compiler_params=pltpu.CompilerParams(vmem_limit_bytes=WHOLE_LIMIT if first_call and last else ABSORB_LIMIT),
        cost_estimate=expected(
            blocks * 2 * times * points * width * planes * lanes, blocks * 2 * width * (points + planes_local * lanes)
        ),
        name="absorb",
    )(*operands)


def transform(received, tables, previous, exchange, total_rows, total_pairs):
    sources, pw_size, pairs, lines, rows, width = received.shape
    number = sources * lines
    line_table, high_table, low_table = tables
    part, first_pair, _ = exchange
    step = 2 if first_pair % 2 == 0 and pairs % 2 == 0 and total_pairs % 2 == 0 else 1
    together = 2

    def kernel(line_ref, high_ref, low_ref, in_ref, *rest):
        out_ref, sides_ref = rest[-2:]
        for pair in range(step):
            images = jnp.swapaxes(in_ref[:, 0, pair].reshape(number, rows, width), 0, 1)
            for first in range(0, rows, together):
                group = range(first, first + together)
                side_by_side = jnp.concatenate([images[r] for r in group], axis=1)
                lined = jnp.dot(line_ref[...], side_by_side, preferred_element_type=jnp.float32)
                for r in group:
                    at, lanes = slice(r * number, (r + 1) * number), slice((r - first) * width, (r - first + 1) * width)
                    sides_ref[at, :width] = lined[:number, lanes]
                    sides_ref[at, width:] = lined[number:, lanes]
            sides = sides_ref[...]
            high = sides.astype(jnp.bfloat16)
            low = (sides - high.astype(jnp.float32)).astype(jnp.bfloat16)
            waves = jnp.dot(high, high_ref[...], preferred_element_type=jnp.float32)
            waves += jnp.dot(low, high_ref[...], preferred_element_type=jnp.float32)
            waves += jnp.dot(high, low_ref[...], preferred_element_type=jnp.float32)
            for plane in range(2):
                lanes = slice(plane * width, (plane + 1) * width)
                out_ref[0, :, 2 * pair + plane] = waves[:, lanes].reshape(rows, number, width)

    out_shape = (1, total_rows, 2 * pw_size * total_pairs, number, width)
    whole = lambda p, j: (0, 0)
    operands = [line_table, high_table, low_table, received]
    in_specs = [
        pl.BlockSpec(line_table.shape, whole),
        pl.BlockSpec(high_table.shape, whole),
        pl.BlockSpec(low_table.shape, whole),
        pl.BlockSpec((sources, 1, step, lines, rows, width), lambda p, j: (0, p, j, 0, 0, 0)),
    ]
    aliases = {}
    if previous is not None:
        aliases = {len(operands): 0}
        operands.append(previous)
        in_specs.append(pl.BlockSpec(memory_space=pl.ANY))
    work = pw_size * pairs * rows * number
    return pl.pallas_call(
        kernel,
        grid=(pw_size, pairs // step),
        in_specs=in_specs,
        out_specs=pl.BlockSpec(
            (1, rows, 2 * step, number, width), lambda p, j: (0, part, (p * total_pairs + first_pair) // step + j, 0, 0)
        ),
        out_shape=jax.ShapeDtypeStruct(out_shape, jnp.float32),
        scratch_shapes=[pltpu.VMEM((rows * number, 2 * width), jnp.float32)],
        input_output_aliases=aliases,
        compiler_params=pltpu.CompilerParams(vmem_limit_bytes=TRANSFORM_LIMIT),
        cost_estimate=expected(work * 2 * width * (2 * number + 6 * width), work * width * 10),
        name="transform",
    )(*operands)


def ring_places(number):
    order = list(range(0, number, 2)) + list(range(number - 1, 0, -2))
    onward = [(order[n], order[(n + 1) % number]) for n in range(number)]
    back = [(to, source) for source, to in onward]
    arrivals = np.zeros((number, number), np.int32)
    for n, device in enumerate(order):
        sequence = [n]
        for hop in range(1, number // 2):
            sequence += [n - hop, n + hop]
        sequence.append(n + number // 2)
        arrivals[device] = [order[m % number] for m in sequence]
    return onward, back, arrivals


def after(arrays, *tokens):
    count = len(arrays)
    anywhere = pl.BlockSpec(memory_space=pl.ANY)
    return pl.pallas_call(
        lambda *refs: None,
        in_specs=[anywhere] * count + [pl.BlockSpec(memory_space=pltpu.VMEM)] * len(tokens),
        out_specs=[anywhere] * count,
        out_shape=[jax.ShapeDtypeStruct(array.shape, array.dtype) for array in arrays],
        input_output_aliases={n: n for n in range(count)},
        compiler_params=pltpu.CompilerParams(vmem_limit_bytes=SMALL_LIMIT),
        name="after",
    )(*arrays, *[pltpu.with_memory_space_constraint(token, pltpu.VMEM) for token in tokens])


def choose(core, first, second):
    shape, dtype = first.shape, first.dtype
    some = (shape[0] // PARTS, shape[1])

    def kernel(core_ref, first_ref, second_ref, out_ref, some_ref):
        for core_index, ref in enumerate((first_ref, second_ref)):

            @pl.when(core_ref[0] == core_index)
            def _():
                out_ref[...] = ref[...]
                some_ref[...] = ref[: some[0]]

    kept = pl.BlockSpec(memory_space=pltpu.VMEM)
    return pl.pallas_call(
        kernel,
        in_specs=[pl.BlockSpec(memory_space=pltpu.SMEM), kept, kept],
        out_specs=[kept, kept],
        out_shape=[pltpu.VMEM(shape, dtype), pltpu.VMEM(some, dtype)],
        compiler_params=pltpu.CompilerParams(vmem_limit_bytes=4 * SMALL_LIMIT),
        name="choose",
    )(core, first, second)


def swapped(rows):
    return [(rows, 0), (lax.ppermute(rows, "tm", SWAP), 1)]


def pick(table, index):
    here = index[..., None] == jnp.arange(table.shape[0], dtype=index.dtype)
    return jnp.sum(jnp.where(here, table, jnp.zeros_like(table)), axis=-1)


def gather_and_absorb(mine, core, places, ring, columns, small, absorb_blocks):
    number = lax.axis_size("grid")
    onward, back = ring
    blocks, every, acc = [swapped(mine)], [], None
    ready, token = prepare(places, number - AHEAD, core, small, columns, EXCHANGES[0])
    tokens = [token]
    up = down = mine
    for hops in range(1, number // 2):
        up, down = lax.ppermute(up, "grid", onward), lax.ppermute(down, "grid", back)
        start = len(every)
        every += blocks
        acc, token = absorb_blocks(blocks, EXCHANGES[0], start, None, acc, False)
        up, down = after([up, down], token, *tokens)
        tokens = []
        blocks = [swapped(up), swapped(down)]
    far, some = choose(core, up, down)
    sides = list(enumerate((onward, back)))
    own, other = [
        lax.ppermute(
            rows, ("grid", "tm"), [(2 * source + side, 2 * to + (side ^ flip)) for side, pairs in sides for source, to in pairs]
        )
        for rows, flip in ((far, 0), (some, 1))
    ]
    start = len(every)
    every += blocks
    acc, token = absorb_blocks(
        blocks, EXCHANGES[0], start, (ready, 0) if AHEAD > len(blocks) else None, acc, False
    )
    own, other = after([own, other], token)
    blocks = [[(own, 0), (other, 1)]]
    _, sent = absorb_blocks(blocks, EXCHANGES[0], number - 1, (ready, AHEAD - 1), acc, True)
    return sent, every + blocks, every + [swapped(own)]


def shards(
    slab_orbitals,
    orbital_block,
    occupied_columns,
    unoccupied_columns,
    occupied_gap,
    unoccupied_gap,
    time_table,
    frequency_table,
    time_weight,
    time_index,
    frequency_index,
):
    grid_size, tm_size, pw_size = (lax.axis_size(axis) for axis in AXES)
    moment = lax.axis_index("tm").astype(jnp.int32)
    core = moment.reshape(1)
    owners = grid_size * pw_size
    rows = SLAB // owners
    part_rows = rows // PARTS

    by_owner = jnp.transpose(slab_orbitals[0]).reshape(owners, PARTS, part_rows, -1)
    by_owner = lax.dynamic_slice_in_dim(by_owner, moment * (owners // tm_size), owners // tm_size, 0)
    onward, back, arrivals = ring_places(grid_size)
    arrivals = jnp.asarray(arrivals)
    mine_first = jnp.arange(grid_size)[:, None] == lax.axis_index("grid")
    places = pick(orbital_block, jnp.sum(jnp.where(mine_first, arrivals, 0), axis=0))

    time_points = pick(time_table, time_index)
    frequency_weights = pick(time_weight, time_index)[None, :] * jnp.cos(
        pick(frequency_table, frequency_index)[:, None] * time_points[None, :]
    )

    columns = (occupied_columns, unoccupied_columns)
    finish = (-frequency_weights, (grid_size, pw_size))

    def absorb_blocks(pieces, exchange, start, ready, acc, last):
        decays = (time_points, occupied_gap, unoccupied_gap)
        return absorb(pieces, exchange, places, start, core, decays, columns, ready, acc, finish, last)

    tables = (jnp.asarray(line_operator(NY)),) + tuple(jnp.asarray(t) for t in row_operator(NX))
    mine = jnp.swapaxes(by_owner, 0, 1).reshape(SLAB // tm_size, -1)
    result = None
    for exchange in EXCHANGES:
        if exchange == EXCHANGES[0]:
            sent, *blocks = gather_and_absorb(mine, core, places, (onward, back), columns, (time_points, finish[0]), absorb_blocks)
        else:
            _, sent = absorb_blocks(blocks[exchange[0]], exchange, 0, None, None, True)
        sent = sent.reshape((-1,) + sent.shape[3:])
        received = lax.all_to_all(sent, AXES, split_axis=0, concat_axis=0, tiled=True)
        received = received.reshape((grid_size * tm_size, pw_size) + received.shape[1:])
        result = transform(received, tables, result, exchange, rows, occupied_columns.shape[1] // 2)
    return result


def solution(mesh):
    placed = (
        P("grid", None, None),
        P(),
        P(None, "pw", "grid"),
        P(None, "pw", "grid"),
        P(),
        P(),
        P(),
        P(),
        P(),
        P(),
        P(),
    )
    rows = SLAB // (mesh.shape["grid"] * mesh.shape["pw"])
    lanes = NX * NY // (mesh.shape["grid"] * mesh.shape["tm"])
    fits = rows % (GROUP * PARTS) == 0 and lanes % 128 == 0
    return jax.shard_map(
        shards if fits else general_shards,
        mesh=mesh,
        in_specs=placed,
        out_specs=P("tm", ("grid", "pw"), None, None, None),
        check_vma=False,
    )
```

```python
import math

import jax
import jax.numpy as jnp
import ml_dtypes
import numpy as np
from jax import lax
from jax.experimental import pallas as pl
from jax.experimental.pallas import tpu as pltpu
from jax.sharding import PartitionSpec as P

NX = 64
NY = 64
SLAB = 512


def dft_angles(number):
    indices = jnp.arange(number, dtype=jnp.int32)
    product = indices[:, None] * indices[None, :] % number
    return product.astype(jnp.float32) * (2.0 * math.pi / number)


def row_table(number):
    angles = dft_angles(number)
    factor = 1.0 / math.sqrt(number)
    return jnp.concatenate([jnp.cos(angles), -jnp.sin(angles)], axis=1) * factor


def column_table(number):
    angles = dft_angles(number)
    factor = 1.0 / math.sqrt(number)
    return (jnp.concatenate([jnp.cos(angles), jnp.sin(angles)], axis=0) * factor).astype(
        jnp.bfloat16
    )


def combine_parts(y_parts, width_y, width_x):
    cosine = y_parts[..., :width_y, :]
    sine = y_parts[..., width_y:, :]
    real_part = cosine[..., :width_x] + sine[..., width_x:]
    imag_part = cosine[..., width_x:] - sine[..., :width_x]
    return jnp.concatenate([real_part, imag_part], axis=-1)


def weigh_rows(values, rates, time_point):
    return (values * jnp.exp(-rates * time_point)[:, :, None]).astype(jnp.bfloat16)


def general_shards(
    slab_orbitals,
    orbital_block,
    occupied_columns,
    unoccupied_columns,
    occupied_gap,
    unoccupied_gap,
    time_table,
    frequency_table,
    time_weight,
    time_index,
    frequency_index,
):
    block_count = lax.axis_size("grid")
    occupied_block = occupied_columns.shape[0] // block_count
    unoccupied_block = unoccupied_columns.shape[0] // block_count
    planes_local = occupied_columns.shape[1]
    lines_local = occupied_columns.shape[2] // NX
    width = planes_local * occupied_columns.shape[2]
    occupied_blocks = occupied_columns.reshape(block_count, occupied_block, width)
    unoccupied_blocks = unoccupied_columns.reshape(block_count, unoccupied_block, width)
    occupied_rates = occupied_gap.reshape(block_count, occupied_block)
    unoccupied_rates = unoccupied_gap.reshape(block_count, unoccupied_block)
    moment = lax.axis_index("tm")
    time_slot = time_index[moment]
    time_point = time_table[time_slot]
    frequency_weights = time_weight[time_slot] * jnp.cos(
        frequency_table[frequency_index] * time_point
    )
    pieces = lax.all_gather(slab_orbitals, "grid", axis=0, tiled=True)
    occupied_part = weigh_rows(
        pieces[:, :occupied_block, :], jnp.take(occupied_rates, orbital_block, axis=0), time_point
    )
    unoccupied_part = weigh_rows(
        pieces[:, occupied_block:, :], jnp.take(unoccupied_rates, orbital_block, axis=0), time_point
    )
    green_occupied = jnp.einsum(
        "jis,jic->sc",
        occupied_part,
        jnp.take(occupied_blocks, orbital_block, axis=0),
        preferred_element_type=jnp.float32,
    )
    green_unoccupied = jnp.einsum(
        "jis,jic->sc",
        unoccupied_part,
        jnp.take(unoccupied_blocks, orbital_block, axis=0),
        preferred_element_type=jnp.float32,
    )
    green_occupied, green_unoccupied = (green_occupied, green_unoccupied)
    response = -green_occupied * green_unoccupied
    response = response.reshape(SLAB, planes_local, lines_local, NX)
    tiles = jnp.dot(response, row_table(NX), precision=lax.Precision.HIGHEST).astype(jnp.bfloat16)
    y_table = column_table(NY)
    received = lax.all_to_all(
        tiles[:, None], ("grid", "pw"), split_axis=0, concat_axis=1, tiled=True
    )
    stacked = received[None]
    sources = stacked.reshape(
        stacked.shape[0],
        stacked.shape[1],
        block_count,
        lax.axis_size("pw"),
        planes_local,
        lines_local,
        2 * NX,
    )
    y_parts = jnp.einsum(
        "kgy,trgpzyc->trpzkc",
        y_table.reshape(2 * NY, block_count, lines_local),
        sources,
        preferred_element_type=jnp.float32,
    )
    y_parts = y_parts.reshape(
        y_parts.shape[0], y_parts.shape[1], lax.axis_size("pw") * planes_local, 2 * NY, 2 * NX
    )
    plane_waves = combine_parts(y_parts, NY, NX)
    summed = lax.psum(frequency_weights[:, None, None, None, None] * plane_waves[0][None], "tm")
    return lax.dynamic_slice_in_dim(summed, moment, 1, 0)


PARTS = 2
EXCHANGES = ((0, 0, 4), (1, 0, 4))
AHEAD = 1
TURN = 64
GROUP = 16
ABSORB_LIMIT = 16 * 2**20
WHOLE_LIMIT = 28 * 2**20
TRANSFORM_LIMIT = 24 * 2**20
SMALL_LIMIT = 2**20
AXES = ("grid", "tm", "pw")
SWAP = [(0, 1), (1, 0)]
TOKEN = jax.ShapeDtypeStruct((8, 128), jnp.float32)


def host_angles(number):
    indices = np.arange(number)
    return (indices[:, None] * indices[None, :] % number) * (2.0 * math.pi / number)


def line_operator(lines):
    angles = host_angles(lines)
    table = np.concatenate([np.cos(angles), np.sin(angles)]) / math.sqrt(lines)
    return table.astype(np.float32).astype(ml_dtypes.bfloat16)


def row_operator(number):
    angles = host_angles(number)
    cosine, sine = np.cos(angles) / math.sqrt(number), np.sin(angles) / math.sqrt(number)
    one = np.stack([np.concatenate([cosine, -sine], 1), np.concatenate([-sine, -cosine], 1)])
    both = np.einsum("sxc,pq->spxqc", one, np.eye(2)).reshape(4 * number, 4 * number)
    high = both.astype(np.float32).astype(ml_dtypes.bfloat16)
    low = (both - high.astype(np.float64)).astype(np.float32).astype(ml_dtypes.bfloat16)
    return high, low


def expected(flops, read_and_written):
    return pl.CostEstimate(flops=flops, bytes_accessed=read_and_written, transcendentals=0)


def hbm(array):
    return pltpu.with_memory_space_constraint(array, pltpu.HBM)


def take_planes(block_ref, out_ref, row, first):
    planes = out_ref.shape[0]
    for start in range(0, block_ref.shape[0], TURN):
        turned = jnp.swapaxes(block_ref[start : start + TURN], 0, 1)
        out_ref[:, row + start : row + start + TURN] = turned[first : first + planes]


def column_specs(columns, blocks, start):
    return [
        pl.BlockSpec(
            (array.shape[0] // blocks, array.shape[1], array.shape[2] // 2), lambda n, place, core: (place[start + n], 0, core[0])
        )
        for array in columns
    ]


def prepare(places, start, core, small, columns, exchange):
    _, first_pair, pairs = exchange
    blocks = places.shape[0]
    count = blocks - start
    occupied_block = columns[0].shape[0] // blocks
    width = occupied_block + columns[1].shape[0] // blocks
    shape = (count, 2 * pairs, width, columns[0].shape[2] // 2)

    def kernel(place_ref, core_ref, *refs):
        occ_col, unocc_col, ready_ref, token_ref = refs[len(small) :]
        here = ready_ref.at[pl.program_id(0)]
        take_planes(occ_col, here, 0, 2 * first_pair)
        take_planes(unocc_col, here, occupied_block, 2 * first_pair)
        token_ref[...] = jnp.zeros_like(token_ref)

    return pl.pallas_call(
        kernel,
        grid_spec=pltpu.PrefetchScalarGridSpec(
            num_scalar_prefetch=2,
            grid=(count,),
            in_specs=[pl.BlockSpec(memory_space=pltpu.SMEM)] * len(small) + column_specs(columns, blocks, start),
            out_specs=[pl.BlockSpec(memory_space=pltpu.VMEM), pl.BlockSpec(TOKEN.shape, lambda n, place, core: (0, 0))],
        ),
        out_shape=[pltpu.VMEM(shape, jnp.bfloat16), pltpu.VMEM(TOKEN.shape, TOKEN.dtype)],
        compiler_params=pltpu.CompilerParams(vmem_limit_bytes=16 * SMALL_LIMIT),
        cost_estimate=expected(0, 2 * math.prod(shape)),
        name="prepare",
    )(places, core, *small, *[hbm(array) for array in columns])


def mix_response(weight_ref, acc_ref, out_ref):
    _, planes, _, width = acc_ref.shape
    grid_size, times, pw_size, _, lines, rows, _ = out_ref.shape
    points = grid_size * pw_size * rows
    for pair in range(planes // 2):
        mixed = []
        for z in (2 * pair, 2 * pair + 1):
            product = acc_ref[0, z] * acc_ref[1, z]
            first, second = product[:points], product[points:]
            mixed.append([
                (weight_ref[f, 0] * first + weight_ref[f, 1] * second).astype(jnp.bfloat16) for f in range(times)
            ])
        for f in range(times):
            even, odd = mixed[0][f], mixed[1][f]
            for y in range(lines):
                at = slice(y * NX, (y + 1) * NX)
                both = jnp.concatenate([even[:, at], odd[:, at]], axis=1)
                out_ref[:, f, :, pair, y] = both.reshape(grid_size, pw_size, rows, 2 * NX)


def absorb(pieces, exchange, places, start, core, decays, columns, ready, acc, finish, last):
    time_points, occupied_gap, unoccupied_gap = decays
    occupied_columns, unoccupied_columns = columns
    times, occupied_count = time_points.shape[0], occupied_gap.shape[0]
    unoccupied_count = unoccupied_gap.shape[0]
    part, first_pair, pairs = exchange
    planes, planes_local, lanes = 2 * pairs, occupied_columns.shape[1], occupied_columns.shape[2] // 2
    flat = [entry for block in pieces for entry in block]
    width = flat[0][0].shape[1]
    half = SLAB // 2 // PARTS
    points = 2 * half
    occupied_block = occupied_count * width // (occupied_count + unoccupied_count)
    unoccupied_block = width - occupied_block
    first_call = acc is None
    blocks = len(pieces)

    def kernel(place_ref, core_ref, time_ref, occ_ref, unocc_ref, *rest):
        col_refs, rest = rest[: 2 if ready is None else 1], rest[2 if ready is None else 1 :]
        refs, rest = rest[: len(flat)], rest[len(flat) :]
        if not first_call:
            rest = rest[1:]
        weight_ref, acc_ref, last_ref, weighed, *taken = rest
        if ready is None:
            (taken,) = taken
            take_planes(col_refs[0], taken, 0, 2 * first_pair)
            take_planes(col_refs[1], taken, occupied_block, 2 * first_pair)
        else:
            taken = col_refs[0].at[ready[1] + pl.program_id(0)]
        factors = [
            [jnp.exp(-ref[...] * time_ref[t]) for ref in (occ_ref, unocc_ref)] for t in range(times)
        ]
        for n, block in enumerate(pieces):
            mine, refs = refs[: len(block)], refs[len(block) :]

            @pl.when(pl.program_id(0) == n)
            def _():
                for ref, (_, other) in zip(mine, block):
                    side = 1 - core_ref[0] if other else core_ref[0]
                    values = ref[...].astype(jnp.float32)
                    for t in range(times):
                        at = pl.ds(pl.multiple_of(t * points + side * half, half), half)
                        for low, high, factor in ((0, occupied_block, factors[t][0]), (occupied_block, width, factors[t][1])):
                            weighed[at, low:high] = (values[:, low:high] * factor).astype(jnp.bfloat16)

        if first_call and blocks > 1:

            @pl.when(pl.program_id(0) == 0)
            def _():
                acc_ref[...] = jnp.zeros_like(acc_ref)

        for kind, at in enumerate((slice(0, occupied_block), slice(occupied_block, width))):
            for z in range(planes):
                part_sum = jnp.dot(weighed[:, at], taken[z, at], preferred_element_type=jnp.float32)
                if first_call and blocks == 1:
                    acc_ref[kind, z] = part_sum
                else:
                    acc_ref[kind, z] += part_sum

        if last:

            @pl.when(pl.program_id(0) == len(pieces) - 1)
            def _():
                mix_response(weight_ref, acc_ref, last_ref)

        else:
            last_ref[...] = jnp.zeros_like(last_ref)

    total = (2, planes, times * points, lanes)
    kept = pl.BlockSpec(memory_space=pltpu.VMEM)
    operands = [places, core, time_points, occupied_gap.reshape(1, -1), unoccupied_gap.reshape(1, -1)]
    if ready is None:
        operands += [hbm(occupied_columns), hbm(unoccupied_columns)]
        column_in = column_specs(columns, places.shape[0], start)
    else:
        operands.append(pltpu.with_memory_space_constraint(ready[0], pltpu.VMEM))
        column_in = [kept]
    operands += [hbm(entry[0]) if first_call and last else entry[0] for entry in flat]
    in_specs = [
        pl.BlockSpec(memory_space=pltpu.SMEM),
        pl.BlockSpec((1, occupied_block), lambda n, place, core: (0, place[start + n])),
        pl.BlockSpec((1, unoccupied_block), lambda n, place, core: (0, place[start + n])),
        *column_in,
    ] + [pl.BlockSpec((half, width), lambda n, place, core: (part, 0)) for entry in flat]
    out_specs, out_shape, aliases = [kept], [pltpu.VMEM(total, jnp.float32)], {}
    if not first_call:
        aliases = {len(operands): 0}
        operands.append(acc)
        in_specs.append(kept)
    weights, (grid_size, pw_size) = finish
    operands.append(weights)
    in_specs.append(pl.BlockSpec(memory_space=pltpu.SMEM))
    if last:
        rows = points // (grid_size * pw_size)
        sent = (grid_size, times, pw_size, planes // 2, lanes // NX, rows, 2 * NX)
        out_specs.append(pl.BlockSpec(sent, lambda n, place, core: (0,) * len(sent)))
        out_shape.append(pltpu.HBM(sent, jnp.bfloat16))
    else:
        out_specs.append(pl.BlockSpec(TOKEN.shape, lambda n, place, core: (0, 0)))
        out_shape.append(pltpu.VMEM(TOKEN.shape, TOKEN.dtype))
    return pl.pallas_call(
        kernel,
        grid_spec=pltpu.PrefetchScalarGridSpec(
            num_scalar_prefetch=2,
            grid=(blocks,),
            in_specs=in_specs,
            out_specs=out_specs,
            scratch_shapes=[
                pltpu.VMEM((times * points, width), jnp.bfloat16),
            ]
            + ([pltpu.VMEM((planes, width, lanes), jnp.bfloat16)] if ready is None else []),
        ),
        out_shape=out_shape,
        input_output_aliases=aliases,
        compiler_params=pltpu.CompilerParams(vmem_limit_bytes=WHOLE_LIMIT if first_call and last else ABSORB_LIMIT),
        cost_estimate=expected(
            blocks * 2 * times * points * width * planes * lanes, blocks * 2 * width * (points + planes_local * lanes)
        ),
        name="absorb",
    )(*operands)


def transform(received, tables, previous, exchange, total_rows, total_pairs):
    sources, pw_size, pairs, lines, rows, width = received.shape
    number = sources * lines
    line_table, high_table, low_table = tables
    part, first_pair, _ = exchange
    step = 2 if first_pair % 2 == 0 and pairs % 2 == 0 and total_pairs % 2 == 0 else 1
    together = 2

    def kernel(line_ref, high_ref, low_ref, in_ref, *rest):
        out_ref, sides_ref = rest[-2:]
        for pair in range(step):
            images = jnp.swapaxes(in_ref[:, 0, pair].reshape(number, rows, width), 0, 1)
            for first in range(0, rows, together):
                group = range(first, first + together)
                side_by_side = jnp.concatenate([images[r] for r in group], axis=1)
                lined = jnp.dot(line_ref[...], side_by_side, preferred_element_type=jnp.float32)
                for r in group:
                    at, lanes = slice(r * number, (r + 1) * number), slice((r - first) * width, (r - first + 1) * width)
                    sides_ref[at, :width] = lined[:number, lanes]
                    sides_ref[at, width:] = lined[number:, lanes]
            sides = sides_ref[...]
            high = sides.astype(jnp.bfloat16)
            low = (sides - high.astype(jnp.float32)).astype(jnp.bfloat16)
            waves = jnp.dot(high, high_ref[...], preferred_element_type=jnp.float32)
            waves += jnp.dot(low, high_ref[...], preferred_element_type=jnp.float32)
            waves += jnp.dot(high, low_ref[...], preferred_element_type=jnp.float32)
            for plane in range(2):
                lanes = slice(plane * width, (plane + 1) * width)
                out_ref[0, :, 2 * pair + plane] = waves[:, lanes].reshape(rows, number, width)

    out_shape = (1, total_rows, 2 * pw_size * total_pairs, number, width)
    whole = lambda p, j: (0, 0)
    operands = [line_table, high_table, low_table, received]
    in_specs = [
        pl.BlockSpec(line_table.shape, whole),
        pl.BlockSpec(high_table.shape, whole),
        pl.BlockSpec(low_table.shape, whole),
        pl.BlockSpec((sources, 1, step, lines, rows, width), lambda p, j: (0, p, j, 0, 0, 0)),
    ]
    aliases = {}
    if previous is not None:
        aliases = {len(operands): 0}
        operands.append(previous)
        in_specs.append(pl.BlockSpec(memory_space=pl.ANY))
    work = pw_size * pairs * rows * number
    return pl.pallas_call(
        kernel,
        grid=(pw_size, pairs // step),
        in_specs=in_specs,
        out_specs=pl.BlockSpec(
            (1, rows, 2 * step, number, width), lambda p, j: (0, part, (p * total_pairs + first_pair) // step + j, 0, 0)
        ),
        out_shape=jax.ShapeDtypeStruct(out_shape, jnp.float32),
        scratch_shapes=[pltpu.VMEM((rows * number, 2 * width), jnp.float32)],
        input_output_aliases=aliases,
        compiler_params=pltpu.CompilerParams(vmem_limit_bytes=TRANSFORM_LIMIT),
        cost_estimate=expected(work * 2 * width * (2 * number + 6 * width), work * width * 10),
        name="transform",
    )(*operands)


def ring_places(number):
    order = list(range(0, number, 2)) + list(range(number - 1, 0, -2))
    onward = [(order[n], order[(n + 1) % number]) for n in range(number)]
    back = [(to, source) for source, to in onward]
    arrivals = np.zeros((number, number), np.int32)
    for n, device in enumerate(order):
        sequence = [n]
        for hop in range(1, number // 2):
            sequence += [n - hop, n + hop]
        sequence.append(n + number // 2)
        arrivals[device] = [order[m % number] for m in sequence]
    return onward, back, arrivals


def after(arrays, *tokens):
    count = len(arrays)
    anywhere = pl.BlockSpec(memory_space=pl.ANY)
    return pl.pallas_call(
        lambda *refs: None,
        in_specs=[anywhere] * count + [pl.BlockSpec(memory_space=pltpu.VMEM)] * len(tokens),
        out_specs=[anywhere] * count,
        out_shape=[jax.ShapeDtypeStruct(array.shape, array.dtype) for array in arrays],
        input_output_aliases={n: n for n in range(count)},
        compiler_params=pltpu.CompilerParams(vmem_limit_bytes=SMALL_LIMIT),
        name="after",
    )(*arrays, *[pltpu.with_memory_space_constraint(token, pltpu.VMEM) for token in tokens])


def choose(core, first, second):
    shape, dtype = first.shape, first.dtype
    some = (shape[0] // PARTS, shape[1])

    def kernel(core_ref, first_ref, second_ref, out_ref, some_ref):
        for core_index, ref in enumerate((first_ref, second_ref)):

            @pl.when(core_ref[0] == core_index)
            def _():
                out_ref[...] = ref[...]
                some_ref[...] = ref[: some[0]]

    kept = pl.BlockSpec(memory_space=pltpu.VMEM)
    return pl.pallas_call(
        kernel,
        in_specs=[pl.BlockSpec(memory_space=pltpu.SMEM), kept, kept],
        out_specs=[kept, kept],
        out_shape=[pltpu.VMEM(shape, dtype), pltpu.VMEM(some, dtype)],
        compiler_params=pltpu.CompilerParams(vmem_limit_bytes=4 * SMALL_LIMIT),
        name="choose",
    )(core, first, second)


def swapped(rows):
    return [(rows, 0), (lax.ppermute(rows, "tm", SWAP), 1)]


def pick(table, index):
    here = index[..., None] == jnp.arange(table.shape[0], dtype=index.dtype)
    return jnp.sum(jnp.where(here, table, jnp.zeros_like(table)), axis=-1)


def gather_and_absorb(mine, core, places, ring, columns, small, absorb_blocks):
    number = lax.axis_size("grid")
    onward, back = ring
    blocks, every, acc = [swapped(mine)], [], None
    ready, token = prepare(places, number - AHEAD, core, small, columns, EXCHANGES[0])
    tokens = [token]
    up = down = mine
    for hops in range(1, number // 2):
        up, down = lax.ppermute(up, "grid", onward), lax.ppermute(down, "grid", back)
        start = len(every)
        every += blocks
        acc, token = absorb_blocks(blocks, EXCHANGES[0], start, None, acc, False)
        up, down = after([up, down], token, *tokens)
        tokens = []
        blocks = [swapped(up), swapped(down)]
    far, some = choose(core, up, down)
    sides = list(enumerate((onward, back)))
    own, other = [
        lax.ppermute(
            rows, ("grid", "tm"), [(2 * source + side, 2 * to + (side ^ flip)) for side, pairs in sides for source, to in pairs]
        )
        for rows, flip in ((far, 0), (some, 1))
    ]
    start = len(every)
    every += blocks
    acc, token = absorb_blocks(
        blocks, EXCHANGES[0], start, (ready, 0) if AHEAD > len(blocks) else None, acc, False
    )
    own, other = after([own, other], token)
    blocks = [[(own, 0), (other, 1)]]
    _, sent = absorb_blocks(blocks, EXCHANGES[0], number - 1, (ready, AHEAD - 1), acc, True)
    return sent, every + blocks, every + [swapped(own)]


def shards(
    slab_orbitals,
    orbital_block,
    occupied_columns,
    unoccupied_columns,
    occupied_gap,
    unoccupied_gap,
    time_table,
    frequency_table,
    time_weight,
    time_index,
    frequency_index,
):
    grid_size, tm_size, pw_size = (lax.axis_size(axis) for axis in AXES)
    moment = lax.axis_index("tm").astype(jnp.int32)
    core = moment.reshape(1)
    owners = grid_size * pw_size
    rows = SLAB // owners
    part_rows = rows // PARTS

    by_owner = jnp.transpose(slab_orbitals[0]).reshape(owners, PARTS, part_rows, -1)
    by_owner = lax.dynamic_slice_in_dim(by_owner, moment * (owners // tm_size), owners // tm_size, 0)
    onward, back, arrivals = ring_places(grid_size)
    arrivals = jnp.asarray(arrivals)
    mine_first = jnp.arange(grid_size)[:, None] == lax.axis_index("grid")
    places = pick(orbital_block, jnp.sum(jnp.where(mine_first, arrivals, 0), axis=0))

    time_points = pick(time_table, time_index)
    frequency_weights = pick(time_weight, time_index)[None, :] * jnp.cos(
        pick(frequency_table, frequency_index)[:, None] * time_points[None, :]
    )

    columns = (occupied_columns, unoccupied_columns)
    finish = (-frequency_weights, (grid_size, pw_size))

    def absorb_blocks(pieces, exchange, start, ready, acc, last):
        decays = (time_points, occupied_gap, unoccupied_gap)
        return absorb(pieces, exchange, places, start, core, decays, columns, ready, acc, finish, last)

    tables = (jnp.asarray(line_operator(NY)),) + tuple(jnp.asarray(t) for t in row_operator(NX))
    mine = jnp.swapaxes(by_owner, 0, 1).reshape(SLAB // tm_size, -1)
    result = None
    for exchange in EXCHANGES:
        if exchange == EXCHANGES[0]:
            sent, *blocks = gather_and_absorb(mine, core, places, (onward, back), columns, (time_points, finish[0]), absorb_blocks)
        else:
            _, sent = absorb_blocks(blocks[exchange[0]], exchange, 0, None, None, True)
        sent = sent.reshape((-1,) + sent.shape[3:])
        received = lax.all_to_all(sent, AXES, split_axis=0, concat_axis=0, tiled=True)
        received = received.reshape((grid_size * tm_size, pw_size) + received.shape[1:])
        result = transform(received, tables, result, exchange, rows, occupied_columns.shape[1] // 2)
    return result


def solution(mesh):
    placed = (
        P("grid", None, None),
        P(),
        P(None, "pw", "grid"),
        P(None, "pw", "grid"),
        P(),
        P(),
        P(),
        P(),
        P(),
        P(),
        P(),
    )
    rows = SLAB // (mesh.shape["grid"] * mesh.shape["pw"])
    lanes = NX * NY // (mesh.shape["grid"] * mesh.shape["tm"])
    fits = rows % (GROUP * PARTS) == 0 and lanes % 128 == 0
    return jax.shard_map(
        shards if fits else general_shards,
        mesh=mesh,
        in_specs=placed,
        out_specs=P("tm", ("grid", "pw"), None, None, None),
        check_vma=False,
    )
```
